512 devices in a mesh: head: 4 (over x), pb: 8 (over z), kv: 16 (over y, core).
Axes of the slice: x: 4, y: 8, z: 8, core: 2. Of those that a mesh axis runs over, the one named last changes fastest.
Arguments:
- queries: bfloat16 [16384, 4096], P(('pb', 'kv'), 'head'), may hold values from -32 to 32
- keys: bfloat16 [16384, 1024], P(('pb', 'kv'), 'head'), may hold values from -32 to 32
- values: bfloat16 [16384, 1024], P(('pb', 'kv'), 'head'), may hold values from -6 to 6
- doc_lengths: int32 [17], replicated, may hold values from 1 to 1920, 16384 in all
- page_table: int32 [1024], replicated, may hold values from 0 to 1023, as said below
Outputs:
- attended: bfloat16 [16384, 4096], P(('pb', 'kv'), 'head')
- page_pool: bfloat16 [1024, 2, 16, 1024], P(('head', 'pb', 'kv'))
The draws below stay inside these ranges and needn't reach their ends.
Inputs may be any that keep to these rules, and one draw needn't show every extreme that they name: `page_table`: each page number appears once. Slot s holds one of the pages b * 128 to (b + 1) * 128 - 1, where b = (s % 256) // 32.
All inputs are finite; a program needn't handle non-finite values.
Results may differ from the reference program's by a relative error of at most 0.0039.
Values may be sent and summed in bfloat16 or wider, within the bound.
No kernel may reach another device: no remote copies, remote signals or barrier semaphores. Data moves between devices by JAX's collectives and lax.ppermute only.
A program may use at most 64 MiB of HBM per device.

```python
import math
import jax
import jax.numpy as jnp
import numpy as np
from jax import lax

GROUPS = 8
QPG = 4
HD = 128
PAGE = 16
TOKENS = 16384
MOST = 1920
NDOCS = 17
NPAGES = 1024
GROUP_PAGES = 128
HEAD_BLOCK = 256
PB_BLOCK = 32


def draw_queries(key, part):
    key = jax.random.fold_in(key, 11)
    out = 1.7 * jax.random.normal(key, (TOKENS, GROUPS * QPG * HD), jnp.float32)
    return jnp.clip(out, -12.0, 12.0).astype(jnp.bfloat16)


def draw_keys(key, part):
    key = jax.random.fold_in(key, 17)
    out = 1.7 * jax.random.normal(key, (TOKENS, GROUPS * HD), jnp.float32)
    return jnp.clip(out, -12.0, 12.0).astype(jnp.bfloat16)


def draw_page_table(key, part):
    key = jax.random.fold_in(key, 29)
    count = NPAGES // GROUP_PAGES
    orders = jax.vmap(lambda one: jax.random.permutation(one, GROUP_PAGES))(jax.random.split(key, count))
    slots = jnp.arange(NPAGES, dtype=jnp.int32)
    owner = slots % HEAD_BLOCK // PB_BLOCK
    within = slots // HEAD_BLOCK * PB_BLOCK + slots % PB_BLOCK
    return (owner * GROUP_PAGES + orders[owner, within]).astype(jnp.int32)


def steps_of(stream_key, shape, shards, low, largest):
    factor_of, own = 1.0, jax.random.fold_in(stream_key, 6)
    for axis_at, blocks in shards:
        steps = jnp.exp(jax.random.uniform(jax.random.fold_in(own, axis_at), (blocks,), jnp.float32, low / len(shards), largest / len(shards)))
        factor_of = factor_of * jnp.repeat(steps, shape[axis_at] // blocks).reshape([-1 if axis == axis_at else 1 for axis in range(len(shape))])
    return factor_of


def profile(number_of, total, limit, skew):
    weights = [(1 << 20) // math.isqrt(rank ** skew) + 1 for rank in range(2, number_of + 1)]
    rest, given = total - limit - (number_of - 1), [1] * (number_of - 1)
    while rest > 0:
        candidates = [i for i in range(number_of - 1) if given[i] < limit]
        whole, left = sum([weights[i] for i in candidates]), rest
        for i in candidates:
            more = min(limit - given[i], max(1, left * weights[i] // whole), rest)
            given[i] = given[i] + more
            rest = rest - more
    return np.array([limit] + given)


def uneven(own_key, number_of, total, reach, skew):
    if number_of == 2:
        one = jax.random.randint(own_key, (), max(1, total - reach), min(reach, total - 1) + 1)
        return jnp.stack([one, total - one])
    sizes = jnp.asarray(profile(number_of, total, reach, skew), jnp.int32)
    couples = (number_of - 1) // 2
    giver, sink = sizes[1:1 + 2 * couples:2], sizes[2:2 + 2 * couples:2]
    slack = jnp.minimum(giver - 1, reach - sink)
    shifted = jax.random.randint(jax.random.fold_in(own_key, 1), (couples,), 0, 1 << 20) % (slack + 1)
    sizes = sizes.at[1:1 + 2 * couples:2].set(giver - shifted).at[2:2 + 2 * couples:2].set(sink + shifted)
    return sizes[jax.random.permutation(jax.random.fold_in(own_key, 2), number_of)]


def scatter_about(stream_key, dims, deviation, bound, cuts=(), kind=jnp.bfloat16):
    result = deviation * jax.random.normal(stream_key, dims, jnp.float32)
    if cuts:
        result = result * steps_of(stream_key, dims, cuts, -0.22, 0.18)
    return jnp.clip(result, -bound, bound).astype(kind)


def setup_inputs(seed: int = 0) -> dict:
    arg_keys = jax.random.split(jax.random.key(seed), 6)
    return {
        "queries": draw_queries(jax.random.fold_in(arg_keys[5], 71), 0),
        "keys": draw_keys(jax.random.fold_in(arg_keys[5], 71), 0),
        "values": scatter_about(arg_keys[2], (TOKENS, GROUPS * HD), 1.0, 6.0, ((0, 128), (1, 4))),
        "doc_lengths": uneven(arg_keys[3], NDOCS, TOKENS, MOST, 2).astype(jnp.int32),
        "page_table": draw_page_table(jax.random.fold_in(arg_keys[5], 71), 0),
    }


def document_ids(positions, doc_lengths):
    bounds = jnp.cumsum(doc_lengths)
    return jnp.sum((positions[:, None] >= bounds[None, :]).astype(jnp.int32), axis=1)


def reference(queries, keys, values, doc_lengths, page_table):
    scale = HD ** -0.5
    block = math.gcd(TOKENS, 512)
    lead = MOST
    width = MOST + block
    key_pad = jnp.concatenate([jnp.zeros((lead, GROUPS * HD), keys.dtype), keys], axis=0)
    val_pad = jnp.concatenate([jnp.zeros((lead, GROUPS * HD), values.dtype), values], axis=0)
    positions = jnp.arange(TOKENS, dtype=jnp.int32)
    docs = document_ids(positions, doc_lengths)
    docs_pad = jnp.concatenate([jnp.full((lead,), -1, jnp.int32), docs], axis=0)
    grid = queries.reshape(TOKENS, GROUPS, QPG, HD)

    def one_block(index):
        start = (index * block).astype(jnp.int32)
        qblk = lax.dynamic_slice_in_dim(grid, start, block, 0).astype(jnp.float32)
        kblk = lax.dynamic_slice_in_dim(key_pad, start, width, 0).reshape(width, GROUPS, HD).astype(jnp.float32)
        vblk = lax.dynamic_slice_in_dim(val_pad, start, width, 0).reshape(width, GROUPS, HD).astype(jnp.float32)
        kdoc = lax.dynamic_slice_in_dim(docs_pad, start, width, 0)
        qdoc = lax.dynamic_slice_in_dim(docs, start, block, 0)
        kpos = start - lead + jnp.arange(width, dtype=jnp.int32)
        qpos = start + jnp.arange(block, dtype=jnp.int32)
        visible = (kdoc[None, :] == qdoc[:, None]) & (kpos[None, :] <= qpos[:, None]) & (kpos[None, :] >= 0)
        mask = visible[:, None, None, :]
        scores = jnp.einsum("rghd,ngd->rghn", qblk, kblk) * scale
        scores = jnp.where(mask, scores, -1e30)
        top = jnp.max(scores, axis=-1, keepdims=True)
        weights = jnp.where(mask, jnp.exp(scores - top), 0.0)
        total = jnp.sum(weights, axis=-1)
        rounded = lax.optimization_barrier(weights.astype(jnp.bfloat16)).astype(jnp.float32)
        mixed = jnp.einsum("rghn,ngd->rghd", rounded, vblk)
        return (mixed / total[..., None]).astype(jnp.bfloat16)

    outs = lax.map(one_block, jnp.arange(TOKENS // block, dtype=jnp.int32))
    attended = outs.reshape(TOKENS, GROUPS * QPG * HD)
    rows = page_table[:, None] * PAGE + jnp.arange(PAGE, dtype=jnp.int32)[None, :]
    page_pool = jnp.stack([keys[rows], values[rows]], axis=1)
    return attended, page_pool
```

```python
import functools
import math

import jax
import jax.numpy as jnp
from jax import lax
from jax.experimental import pallas as pl
from jax.experimental.pallas import tpu as pltpu
from jax.sharding import PartitionSpec as P

HD = 128
PAGE = 16
LOWEST = -1e30
STAT_ROWS = 16


def doc_start(lengths_ref, position):
    bound = jnp.int32(0)
    start = jnp.zeros_like(position)
    for i in range(lengths_ref.shape[0]):
        bound = bound + lengths_ref[i]
        start = jnp.where(bound <= position, bound, start)
    return start


def scan_keys(lengths_ref, q_ref, mine_ref, other_ref, q_base, k_base, core, acc, top, total):
    rows = q_ref.shape[0]
    half = mine_ref.shape[2]
    width = half // 2
    groups = width // HD
    heads = q_ref.shape[1] // width
    lanes = heads * rows
    factor = HD**-0.5 * math.log2(math.e)
    acc[...] = jnp.zeros_like(acc)
    top[...] = jnp.full_like(top, LOWEST)
    total[...] = jnp.zeros_like(total)
    first_start = doc_start(lengths_ref, q_base)
    last_start = doc_start(lengths_ref, q_base + rows - 1)
    q_pos = q_base + lax.broadcasted_iota(jnp.int32, (1, rows), 1)
    q_start = doc_start(lengths_ref, q_pos)

    def step(chip, masked):
        base = k_base + chip * 2 * rows
        if masked:
            row = lax.broadcasted_iota(jnp.int32, (2 * rows, rows), 0)
            k_pos = base + jnp.where(row < rows, row + core * rows, row - core * rows)
            seen = (k_pos <= q_pos) & (k_pos >= q_start)
            seen = jnp.concatenate([seen] * heads, axis=1)
        for g in range(groups):
            at = pl.ds(g * lanes, lanes)
            queries = jnp.concatenate(
                [q_ref[:, (g * heads + h) * HD : (g * heads + h + 1) * HD] for h in range(heads)], axis=0
            )
            k_cols = slice(g * HD, (g + 1) * HD)
            v_cols = slice(width + g * HD, width + (g + 1) * HD)
            keys = jnp.concatenate([mine_ref[chip, :, k_cols], other_ref[chip, :, k_cols]], axis=0)
            values = jnp.concatenate([mine_ref[chip, :, v_cols], other_ref[chip, :, v_cols]], axis=0)
            scores = lax.dot_general(keys, queries, (((1,), (1,)), ((), ())), preferred_element_type=jnp.float32)
            scores = scores * factor
            if masked:
                scores = jnp.where(seen, scores, LOWEST)
            old = top[:, at]
            new = jnp.maximum(old, jnp.max(scores, axis=0, keepdims=True))
            weights = jnp.exp2(scores - new)
            if masked:
                weights = jnp.where(seen, weights, 0.0)
            scale = jnp.exp2(old - new)
            top[:, at] = new
            total[:, at] = total[:, at] * scale + jnp.sum(weights, axis=0, keepdims=True)
            mixed = lax.dot_general(
                values, weights.astype(jnp.bfloat16), (((0,), (0,)), ((), ())), preferred_element_type=jnp.float32
            )
            acc[:, at] = acc[:, at] * scale + mixed

    def one(chip, carry):
        low = k_base + chip * 2 * rows
        high = low + 2 * rows - 1
        some = (low <= q_base + rows - 1) & (high >= first_start)
        whole = (high <= q_base) & (low >= last_start)

        @pl.when(whole)
        def _():
            step(chip, False)

        @pl.when(some & jnp.logical_not(whole))
        def _():
            step(chip, True)

        return carry

    lax.fori_loop(0, mine_ref.shape[0], one, 0)


def split_three(value):
    high = value.astype(jnp.bfloat16)
    rest = value - high.astype(jnp.float32)
    middle = rest.astype(jnp.bfloat16)
    low = (rest - middle.astype(jnp.float32)).astype(jnp.bfloat16)
    return [high, middle, low]


def later_kernel(at_ref, lengths_ref, table_ref, q_ref, mine_ref, other_ref, part_ref, pages_ref, acc, top, total):
    pb, kv, n_pb, n_kv, n_head = at_ref[0], at_ref[1], at_ref[2], at_ref[3], at_ref[4]
    core = lax.rem(kv, 2)
    rows = q_ref.shape[0]
    row_tokens = n_kv * rows
    n_slots = pages_ref.shape[0]
    width = pages_ref.shape[3]
    row_pages = row_tokens // PAGE
    slot_rows = row_pages // n_head
    per = n_slots // 4
    for i in range(n_slots):
        slot = (i // per) * (n_pb * slot_rows) + pb * slot_rows + kv * per + i % per
        page = table_ref[slot] - pb * row_pages
        block_pages = rows // PAGE
        block = lax.div(page, block_pages)
        chip = lax.div(block, 2)
        row = pl.multiple_of(lax.rem(page, block_pages) * PAGE, PAGE)
        own = lax.rem(block, 2) == core

        @pl.when(own)
        def _():
            pages_ref[i, 0] = mine_ref[chip, pl.ds(row, PAGE), 0:width]
            pages_ref[i, 1] = mine_ref[chip, pl.ds(row, PAGE), width : 2 * width]

        @pl.when(jnp.logical_not(own))
        def _():
            pages_ref[i, 0] = other_ref[chip, pl.ds(row, PAGE), 0:width]
            pages_ref[i, 1] = other_ref[chip, pl.ds(row, PAGE), width : 2 * width]

    scan_keys(
        lengths_ref, q_ref, mine_ref, other_ref, (pb + 1) * row_tokens + kv * rows, pb * row_tokens, core, acc, top, total
    )
    part_ref[0:HD, :] = (acc[...] / jnp.maximum(total[...], 1e-30)).astype(jnp.bfloat16)
    stats = split_three(top[...]) + split_three(total[...])
    stats.append(jnp.zeros((STAT_ROWS - len(stats), acc.shape[1]), jnp.bfloat16))
    part_ref[HD : HD + STAT_ROWS, :] = jnp.concatenate(stats, axis=0)


def own_kernel(at_ref, lengths_ref, q_ref, mine_ref, other_ref, acc, top, total):
    pb, kv, n_kv = at_ref[0], at_ref[1], at_ref[3]
    core = lax.rem(kv, 2)
    rows = q_ref.shape[0]
    row_tokens = n_kv * rows
    scan_keys(
        lengths_ref, q_ref, mine_ref, other_ref, pb * row_tokens + kv * rows, pb * row_tokens, core, acc, top, total
    )


def join_kernel(acc_ref, top_ref, total_ref, part_ref, out_ref):
    part = part_ref[0:HD, :].astype(jnp.float32)
    stats = part_ref[HD : HD + STAT_ROWS, :].astype(jnp.float32)
    part_top = stats[0:1] + stats[1:2] + stats[2:3]
    part_total = stats[3:4] + stats[4:5] + stats[5:6]
    part_top = jnp.where(part_total > 0.0, part_top, LOWEST)
    top = jnp.maximum(top_ref[...], part_top)
    own = jnp.exp2(top_ref[...] - top)
    weight = jnp.where(part_total > 0.0, jnp.exp2(part_top - top) * part_total, 0.0)
    inverse = 1.0 / (total_ref[...] * own + weight)
    own = own * inverse
    weight = weight * inverse
    rows = out_ref.shape[0]
    for i in range(out_ref.shape[1] // HD):
        at = slice(i * rows, (i + 1) * rows)
        mixed = acc_ref[:, at] * own[:, at] + part[:, at] * weight[:, at]
        out_ref[:, i * HD : (i + 1) * HD] = jnp.transpose(mixed).astype(jnp.bfloat16)


SMEM = pl.BlockSpec(memory_space=pltpu.SMEM)
VMEM = pl.BlockSpec(memory_space=pltpu.VMEM)
PARAMS = pltpu.CompilerParams(vmem_limit_bytes=40 * 1024 * 1024)


def cost(flops, nbytes):
    return pl.CostEstimate(flops=flops, bytes_accessed=nbytes, transcendentals=0)


def body(queries, keys, values, doc_lengths, page_table):
    rows = queries.shape[0]
    n_head = lax.axis_size("head")
    n_pb = lax.axis_size("pb")
    n_kv = lax.axis_size("kv")
    chips = n_kv // 2
    width = keys.shape[1]
    columns = queries.shape[1]
    lanes = columns // HD * rows
    n_slots = rows // PAGE
    at = jnp.stack([lax.axis_index("pb"), lax.axis_index("kv"), n_pb, n_kv, n_head]).astype(jnp.int32)
    later = lax.ppermute(queries, "pb", [(i + 1, i) for i in range(n_pb - 1)])
    both = jnp.concatenate([keys, values], axis=1)
    sent = jnp.broadcast_to(both[None], (chips, *both.shape))
    ring = [[2 * i + core for i in range(chips)] for core in range(2)]
    mine = lax.all_to_all(sent, "kv", 0, 0, tiled=True, axis_index_groups=ring)
    other = lax.ppermute(mine, "kv", [(i, i ^ 1) for i in range(n_kv)])
    flops = 4 * columns * rows * n_kv * rows
    state = [(HD, lanes), (1, lanes), (1, lanes)]
    part, pages = pl.pallas_call(
        later_kernel,
        out_shape=(
            jax.ShapeDtypeStruct((HD + STAT_ROWS, lanes), jnp.bfloat16),
            jax.ShapeDtypeStruct((n_slots, 2, PAGE, width), jnp.bfloat16),
        ),
        in_specs=[SMEM, SMEM, SMEM, VMEM, VMEM, VMEM],
        out_specs=(VMEM, VMEM),
        scratch_shapes=[pltpu.VMEM(shape, jnp.float32) for shape in state],
        compiler_params=PARAMS,
        cost_estimate=cost(flops, 3 << 20),
        name="later_rows",
    )(at, doc_lengths, page_table, later, mine, other)
    back = lax.ppermute(part, "pb", [(i, i + 1) for i in range(n_pb - 1)])
    page_pool = lax.all_to_all(pages, "head", split_axis=0, concat_axis=3, tiled=True)
    own = pl.pallas_call(
        own_kernel,
        out_shape=tuple(jax.ShapeDtypeStruct(shape, jnp.float32) for shape in state),
        in_specs=[SMEM, SMEM, VMEM, VMEM, VMEM],
        out_specs=(VMEM, VMEM, VMEM),
        compiler_params=PARAMS,
        cost_estimate=cost(flops, 3 << 20),
        name="own_row",
    )(at, doc_lengths, queries, mine, other)
    attended = pl.pallas_call(
        join_kernel,
        out_shape=jax.ShapeDtypeStruct((rows, columns), jnp.bfloat16),
        in_specs=[VMEM] * 4,
        out_specs=VMEM,
        compiler_params=PARAMS,
        cost_estimate=cost(1 << 20, 1 << 20),
        name="join_rows",
    )(*own, back)
    return (attended, page_pool)


def solution(mesh):
    in_specs = (P(("pb", "kv"), "head"), P(("pb", "kv"), "head"), P(("pb", "kv"), "head"), P(), P())
    out_specs = (P(("pb", "kv"), "head"), P(("head", "pb", "kv"), None, None, None))
    return jax.shard_map(body, mesh=mesh, in_specs=in_specs, out_specs=out_specs, check_vma=False)
```

```python
import math

import jax
import jax.numpy as jnp
from jax import lax
from jax.experimental import pallas as pl
from jax.experimental.pallas import tpu as pltpu
from jax.sharding import PartitionSpec as P

HD = 128
PAGE = 16
SPAN = 2
LOWEST = -1e30
STAT_ROWS = 16
FACTOR = HD**-0.5 * math.log2(math.e)


def doc_start(lengths_ref, position):
    bound = jnp.int32(0)
    start = jnp.zeros_like(position)
    for i in range(lengths_ref.shape[0]):
        bound = bound + lengths_ref[i]
        start = jnp.where(bound <= position, bound, start)
    return start


def turn_kernel(*refs):
    for q_ref, out_ref in zip(refs[: len(refs) // 2], refs[len(refs) // 2 :], strict=True):
        rows = q_ref.shape[0]
        for i in range(q_ref.shape[1] // HD):
            out_ref[:, i * rows : (i + 1) * rows] = jnp.transpose(q_ref[:, i * HD : (i + 1) * HD])


def scan_keys(lengths_ref, q_ref, mine_ref, other_ref, q_base, k_base, core, acc, top, total, kept):
    rows = mine_ref.shape[1]
    width = mine_ref.shape[2] // 2
    groups = width // HD
    lanes = q_ref.shape[1] // groups
    heads = lanes // rows
    tile = 2 * rows * SPAN
    count = mine_ref.shape[0] // SPAN
    acc[...] = jnp.zeros_like(acc)
    top[...] = jnp.full_like(top, LOWEST)
    total[...] = jnp.zeros_like(total)
    first_start = doc_start(lengths_ref, q_base)
    last_start = doc_start(lengths_ref, q_base + rows - 1)
    q_pos = q_base + lax.broadcasted_iota(jnp.int32, (1, rows), 1)
    q_start = doc_start(lengths_ref, q_pos)
    low_tile = jnp.clip(lax.div(first_start - k_base, tile), 0, count)
    high_tile = jnp.clip(lax.div(q_base + rows - 1 - k_base, tile) + 1, 0, count)

    def columns(at, cols):
        parts = []
        for chip in range(SPAN):
            parts += [mine_ref[at * SPAN + chip, :, cols], other_ref[at * SPAN + chip, :, cols]]
        return jnp.concatenate(parts, axis=0)

    def score(at, masked):
        if masked:
            row = lax.broadcasted_iota(jnp.int32, (2 * rows, rows), 0)
            k_pos = k_base + at * tile + jnp.where(row < rows, row + core * rows, row - core * rows)
            k_pos = jnp.concatenate([k_pos + chip * 2 * rows for chip in range(SPAN)], axis=0)
            seen = (k_pos <= q_pos) & (k_pos >= q_start)
            seen = jnp.concatenate([seen] * heads, axis=1)
        for g in range(groups):
            where = slice(g * lanes, (g + 1) * lanes)
            keys = columns(at, slice(g * HD, (g + 1) * HD))
            scores = jnp.dot(keys, q_ref[:, where], preferred_element_type=jnp.float32)
            if masked:
                scores = jnp.where(seen, scores, LOWEST)
            kept[at, g] = scores
            top[:, where] = jnp.maximum(top[:, where], jnp.max(scores, axis=0, keepdims=True))

    def first_pass(at, carry):
        low = k_base + at * tile
        whole = (low + tile - 1 <= q_base) & (low >= last_start)

        @pl.when(whole)
        def _():
            score(at, False)

        @pl.when(jnp.logical_not(whole))
        def _():
            score(at, True)

        return carry

    def second_pass(at, carry):
        for g in range(groups):
            where = slice(g * lanes, (g + 1) * lanes)
            peak = jnp.maximum(top[:, where], 0.1 * LOWEST) * FACTOR
            weights = jnp.exp2(kept[at, g] * FACTOR - peak)
            total[:, where] = total[:, where] + jnp.sum(weights, axis=0, keepdims=True)
            values = columns(at, slice(width + g * HD, width + (g + 1) * HD))
            acc[:, where] = acc[:, where] + lax.dot_general(
                values, weights.astype(jnp.bfloat16), (((0,), (0,)), ((), ())), preferred_element_type=jnp.float32
            )
        return carry

    lax.fori_loop(low_tile, high_tile, first_pass, 0)
    lax.fori_loop(low_tile, high_tile, second_pass, 0)


def split_three(value):
    high = value.astype(jnp.bfloat16)
    rest = value - high.astype(jnp.float32)
    middle = rest.astype(jnp.bfloat16)
    low = (rest - middle.astype(jnp.float32)).astype(jnp.bfloat16)
    return [high, middle, low]


def later_kernel(at_ref, lengths_ref, q_ref, mine_ref, other_ref, part_ref, acc, top, total, kept):
    pb, kv, n_kv = at_ref[0], at_ref[1], at_ref[3]
    rows = mine_ref.shape[1]
    row_tokens = n_kv * rows
    scan_keys(
        lengths_ref, q_ref, mine_ref, other_ref, (pb + 1) * row_tokens + kv * rows, pb * row_tokens, lax.rem(kv, 2),
        acc, top, total, kept,
    )
    part_ref[0:HD, :] = (acc[...] / jnp.maximum(total[...], 1e-30)).astype(jnp.bfloat16)
    stats = split_three(top[...]) + split_three(total[...])
    stats.append(jnp.zeros((STAT_ROWS - len(stats), acc.shape[1]), jnp.bfloat16))
    part_ref[HD : HD + STAT_ROWS, :] = jnp.concatenate(stats, axis=0)


def own_kernel(at_ref, lengths_ref, q_ref, mine_ref, other_ref, acc, top, total, kept):
    pb, kv, n_kv = at_ref[0], at_ref[1], at_ref[3]
    rows = mine_ref.shape[1]
    row_tokens = n_kv * rows
    scan_keys(
        lengths_ref, q_ref, mine_ref, other_ref, pb * row_tokens + kv * rows, pb * row_tokens, lax.rem(kv, 2),
        acc, top, total, kept,
    )


def pick_kernel(at_ref, table_ref, mine_ref, other_ref, pages_ref):
    pb, kv, n_pb, n_kv, n_head = at_ref[0], at_ref[1], at_ref[2], at_ref[3], at_ref[4]
    core = lax.rem(kv, 2)
    rows = mine_ref.shape[1]
    n_slots = pages_ref.shape[0]
    width = pages_ref.shape[3]
    row_pages = n_kv * rows // PAGE
    slot_rows = row_pages // n_head
    per = n_slots // 4
    for i in range(n_slots):
        slot = (i // per) * (n_pb * slot_rows) + pb * slot_rows + kv * per + i % per
        page = table_ref[slot] - pb * row_pages
        block_pages = rows // PAGE
        block = lax.div(page, block_pages)
        chip = lax.div(block, 2)
        row = pl.multiple_of(lax.rem(page, block_pages) * PAGE, PAGE)
        own = lax.rem(block, 2) == core
        for half in range(2):
            cols = slice(half * width, (half + 1) * width)
            pages_ref[i, half] = jnp.where(
                own, mine_ref[chip, pl.ds(row, PAGE), cols], other_ref[chip, pl.ds(row, PAGE), cols]
            )


def join_kernel(acc_ref, top_ref, total_ref, part_ref, pages_ref, out_ref, pool_ref):
    part = part_ref[0:HD, :].astype(jnp.float32)
    stats = part_ref[HD : HD + STAT_ROWS, :].astype(jnp.float32)
    part_top = stats[0:1] + stats[1:2] + stats[2:3]
    part_total = stats[3:4] + stats[4:5] + stats[5:6]
    part_top = jnp.where(part_total > 0.0, part_top, LOWEST)
    top = jnp.maximum(top_ref[...], part_top)
    own = jnp.exp2((top_ref[...] - top) * FACTOR)
    weight = jnp.where(part_total > 0.0, jnp.exp2((part_top - top) * FACTOR) * part_total, 0.0)
    inverse = 1.0 / (total_ref[...] * own + weight)
    own = own * inverse
    weight = weight * inverse
    rows = out_ref.shape[0]
    for i in range(out_ref.shape[1] // HD):
        at = slice(i * rows, (i + 1) * rows)
        mixed = acc_ref[:, at] * own[:, at] + part[:, at] * weight[:, at]
        out_ref[:, i * HD : (i + 1) * HD] = jnp.transpose(mixed).astype(jnp.bfloat16)
    slots = pool_ref.shape[0]
    width = pages_ref.shape[3]
    for i in range(pages_ref.shape[0] // slots):
        pool_ref[:, :, :, i * width : (i + 1) * width] = pages_ref[i * slots : (i + 1) * slots]


SMEM = pl.BlockSpec(memory_space=pltpu.SMEM)
VMEM = pl.BlockSpec(memory_space=pltpu.VMEM)
PARAMS = pltpu.CompilerParams(vmem_limit_bytes=40 * 1024 * 1024)


def call(kernel, out_shape, in_specs, name, flops, scratch=()):
    several = isinstance(out_shape, tuple)
    return pl.pallas_call(
        kernel,
        out_shape=out_shape,
        in_specs=in_specs,
        out_specs=(VMEM,) * len(out_shape) if several else VMEM,
        scratch_shapes=scratch,
        compiler_params=PARAMS,
        cost_estimate=pl.CostEstimate(flops=flops, bytes_accessed=3 << 20, transcendentals=0),
        name=name,
    )


def body(queries, keys, values, doc_lengths, page_table):
    rows = queries.shape[0]
    n_head = lax.axis_size("head")
    n_pb = lax.axis_size("pb")
    n_kv = lax.axis_size("kv")
    chips = n_kv // 2
    width = keys.shape[1]
    columns = queries.shape[1]
    lanes = columns // HD * rows
    n_slots = rows // PAGE
    shape = jax.ShapeDtypeStruct
    at = jnp.stack([lax.axis_index("pb"), lax.axis_index("kv"), n_pb, n_kv, n_head]).astype(jnp.int32)
    later = lax.ppermute(queries, "pb", [(i + 1, i) for i in range(n_pb - 1)])
    both = jnp.concatenate([keys, values], axis=1)
    sent = jnp.broadcast_to(both[None], (chips, *both.shape))
    ring = [[2 * i + core for i in range(chips)] for core in range(2)]
    mine = lax.all_to_all(sent, "kv", 0, 0, tiled=True, axis_index_groups=ring)
    turned, later_turned = call(
        turn_kernel, (shape((HD, lanes), jnp.bfloat16),) * 2, [VMEM] * 2, "turn_queries", 1 << 20
    )(queries, later)
    mine, turned, later_turned = lax.optimization_barrier((mine, turned, later_turned))
    other = lax.ppermute(mine, "kv", [(i, i ^ 1) for i in range(n_kv)])
    flops = 4 * columns * rows * n_kv * rows
    state = [(HD, lanes), (1, lanes), (1, lanes)]
    kept = pltpu.VMEM((chips // SPAN, width // HD, 2 * rows * SPAN, lanes // (width // HD)), jnp.float32)
    part = call(
        later_kernel, shape((HD + STAT_ROWS, lanes), jnp.bfloat16), [SMEM, SMEM, VMEM, VMEM, VMEM], "later_rows", flops,
        [pltpu.VMEM(one, jnp.float32) for one in state] + [kept],
    )(at, doc_lengths, later_turned, mine, other)
    back = lax.ppermute(part, "pb", [(i, i + 1) for i in range(n_pb - 1)])
    pages = call(
        pick_kernel, shape((n_slots, 2, PAGE, width), jnp.bfloat16), [SMEM, SMEM, VMEM, VMEM], "pick_pages", 1 << 20
    )(at, page_table, mine, other)
    arrived = lax.all_to_all(pages, "head", split_axis=0, concat_axis=0, tiled=True)
    own = call(
        own_kernel, tuple(shape(one, jnp.float32) for one in state), [SMEM, SMEM, VMEM, VMEM, VMEM], "own_row", flops, [kept]
    )(at, doc_lengths, turned, mine, other)
    return call(
        join_kernel,
        (shape((rows, columns), jnp.bfloat16), shape((n_slots // n_head, 2, PAGE, n_head * width), jnp.bfloat16)),
        [VMEM] * 5,
        "join_rows",
        1 << 20,
    )(*own, back, arrived)


def solution(mesh):
    in_specs = (P(("pb", "kv"), "head"), P(("pb", "kv"), "head"), P(("pb", "kv"), "head"), P(), P())
    out_specs = (P(("pb", "kv"), "head"), P(("head", "pb", "kv"), None, None, None))
    return jax.shard_map(body, mesh=mesh, in_specs=in_specs, out_specs=out_specs, check_vma=False)
```

```python
import math

import jax
import jax.numpy as jnp
from jax import lax
from jax.experimental import pallas as pl
from jax.experimental.pallas import tpu as pltpu
from jax.sharding import PartitionSpec as P

HD = 128
PAGE = 16
SPAN = 2
LOWEST = -1e30
STAT_ROWS = 16
FACTOR = HD**-0.5 * math.log2(math.e)


def doc_start(lengths_ref, position):
    bound = jnp.int32(0)
    start = jnp.zeros_like(position)
    for i in range(lengths_ref.shape[0]):
        bound = bound + lengths_ref[i]
        start = jnp.where(bound <= position, bound, start)
    return start


def spread_kernel(keys_ref, values_ref, out_ref, both, sems):
    width = keys_ref.shape[1]
    copies = [
        pltpu.make_async_copy(keys_ref, both.at[:, 0:width], sems.at[0]),
        pltpu.make_async_copy(values_ref, both.at[:, width : 2 * width], sems.at[1]),
    ]
    for copy in copies:
        copy.start()
    for copy in copies:
        copy.wait()
    for chip in range(out_ref.shape[0]):
        group = chip % 2 * HD
        out_ref[chip, :, 0:HD] = both[:, group : group + HD]
        out_ref[chip, :, HD : 2 * HD] = both[:, width + group : width + group + HD]


def turn_kernel(at_ref, q_ref, keep_ref, give_ref):
    group = lax.rem(lax.div(at_ref[1], 2), 2)
    rows = q_ref.shape[0]
    heads = keep_ref.shape[1] // rows
    for out_ref, one in ((keep_ref, group), (give_ref, 1 - group)):
        for h in range(heads):
            cols = pl.ds(pl.multiple_of((one * heads + h) * HD, HD), HD)
            out_ref[:, h * rows : (h + 1) * rows] = jnp.transpose(q_ref[:, cols])


def scan_keys(lengths_ref, q_refs, mine_ref, other_ref, q_bases, k_base, core, acc, top, total, kept):
    rows = mine_ref.shape[1]
    lanes = q_refs[0].shape[1]
    heads = lanes // rows
    tile = 2 * rows * SPAN
    count = mine_ref.shape[0] // SPAN
    acc[...] = jnp.zeros_like(acc)
    top[...] = jnp.full_like(top, LOWEST)
    total[...] = jnp.zeros_like(total)
    q_low = jnp.minimum(*q_bases)
    q_high = jnp.maximum(*q_bases) + rows - 1
    first_start = doc_start(lengths_ref, q_low)
    last_start = doc_start(lengths_ref, q_high)
    q_pos = [base + lax.broadcasted_iota(jnp.int32, (1, rows), 1) for base in q_bases]
    q_start = [doc_start(lengths_ref, one) for one in q_pos]
    low_tile = jnp.clip(lax.div(first_start - k_base, tile), 0, count)
    high_tile = jnp.clip(lax.div(q_high - k_base, tile) + 1, 0, count)

    def columns(at, cols):
        parts = []
        for chip in range(SPAN):
            parts += [mine_ref[at * SPAN + chip, :, cols], other_ref[at * SPAN + chip, :, cols]]
        return jnp.concatenate(parts, axis=0)

    def score(at, masked):
        keys = columns(at, slice(0, HD))
        if masked:
            row = lax.broadcasted_iota(jnp.int32, (2 * rows, rows), 0)
            k_pos = k_base + at * tile + jnp.where(row < rows, row + core * rows, row - core * rows)
            k_pos = jnp.concatenate([k_pos + chip * 2 * rows for chip in range(SPAN)], axis=0)
        for i, q_ref in enumerate(q_refs):
            where = slice(i * lanes, (i + 1) * lanes)
            scores = jnp.dot(keys, q_ref[...], preferred_element_type=jnp.float32)
            if masked:
                seen = (k_pos <= q_pos[i]) & (k_pos >= q_start[i])
                scores = jnp.where(jnp.concatenate([seen] * heads, axis=1), scores, LOWEST)
            kept[at, i] = scores
            top[:, where] = jnp.maximum(top[:, where], jnp.max(scores, axis=0, keepdims=True))

    def first_pass(at, carry):
        low = k_base + at * tile
        whole = (low + tile - 1 <= q_low) & (low >= last_start)

        @pl.when(whole)
        def _():
            score(at, False)

        @pl.when(jnp.logical_not(whole))
        def _():
            score(at, True)

        return carry

    def second_pass(at, carry):
        values = columns(at, slice(HD, 2 * HD))
        for i in range(len(q_refs)):
            where = slice(i * lanes, (i + 1) * lanes)
            peak = jnp.maximum(top[:, where], 0.1 * LOWEST) * FACTOR
            weights = jnp.exp2(kept[at, i] * FACTOR - peak)
            total[:, where] = total[:, where] + jnp.sum(weights, axis=0, keepdims=True)
            acc[:, where] = acc[:, where] + lax.dot_general(
                values, weights.astype(jnp.bfloat16), (((0,), (0,)), ((), ())), preferred_element_type=jnp.float32
            )
        return carry

    lax.fori_loop(low_tile, high_tile, first_pass, 0)
    lax.fori_loop(low_tile, high_tile, second_pass, 0)


def split_three(value):
    high = value.astype(jnp.bfloat16)
    rest = value - high.astype(jnp.float32)
    middle = rest.astype(jnp.bfloat16)
    low = (rest - middle.astype(jnp.float32)).astype(jnp.bfloat16)
    return [high, middle, low]


def bases(at_ref, rows, later):
    pb, kv, n_kv = at_ref[0], at_ref[1], at_ref[3]
    row_tokens = n_kv * rows
    chip = lax.div(kv, 2)
    mate = (chip + 1 - 2 * lax.rem(chip, 2)) * 2 + lax.rem(kv, 2)
    q_row = (pb + later) * row_tokens
    return (q_row + kv * rows, q_row + mate * rows), pb * row_tokens, lax.rem(kv, 2)


def later_kernel(at_ref, lengths_ref, q_ref, mate_ref, mine_ref, other_ref, part_ref, acc, top, total, kept):
    q_bases, k_base, core = bases(at_ref, mine_ref.shape[1], 1)
    scan_keys(lengths_ref, (q_ref, mate_ref), mine_ref, other_ref, q_bases, k_base, core, acc, top, total, kept)
    part_ref[0:HD, :] = (acc[...] / jnp.maximum(total[...], 1e-30)).astype(jnp.bfloat16)
    stats = split_three(top[...]) + split_three(total[...])
    stats.append(jnp.zeros((STAT_ROWS - len(stats), acc.shape[1]), jnp.bfloat16))
    part_ref[HD : HD + STAT_ROWS, :] = jnp.concatenate(stats, axis=0)


def own_kernel(at_ref, lengths_ref, q_ref, mate_ref, mine_ref, other_ref, acc, top, total, kept):
    q_bases, k_base, core = bases(at_ref, mine_ref.shape[1], 0)
    scan_keys(lengths_ref, (q_ref, mate_ref), mine_ref, other_ref, q_bases, k_base, core, acc, top, total, kept)


def pick_kernel(at_ref, table_ref, mine_ref, other_ref, pages_ref):
    pb, kv, n_pb, n_kv, n_head = at_ref[0], at_ref[1], at_ref[2], at_ref[3], at_ref[4]
    core = lax.rem(kv, 2)
    rows = mine_ref.shape[1]
    n_slots = pages_ref.shape[0]
    row_pages = n_kv * rows // PAGE
    slot_rows = row_pages // n_head
    per = n_slots // 8
    first_chip = lax.div(kv, 4) * 2
    for i in range(n_slots):
        head, chip, which = i // (2 * per), i // per % 2, i % per
        slot = head * (n_pb * slot_rows) + pb * slot_rows + ((first_chip + chip) * 2 + core) * per + which
        page = table_ref[slot] - pb * row_pages
        block_pages = rows // PAGE
        block = lax.div(page, block_pages)
        held = lax.div(block, 2)
        row = pl.multiple_of(lax.rem(page, block_pages) * PAGE, PAGE)
        own = lax.rem(block, 2) == core
        for half in range(2):
            cols = slice(half * HD, (half + 1) * HD)
            pages_ref[i, half] = jnp.where(
                own, mine_ref[held, pl.ds(row, PAGE), cols], other_ref[held, pl.ds(row, PAGE), cols]
            )


def join_kernel(acc_ref, top_ref, total_ref, part_ref, own_ref, mate_ref):
    part = part_ref[0:HD, :].astype(jnp.float32)
    stats = part_ref[HD : HD + STAT_ROWS, :].astype(jnp.float32)
    part_total = stats[3:4] + stats[4:5] + stats[5:6]
    part_top = jnp.where(part_total > 0.0, stats[0:1] + stats[1:2] + stats[2:3], LOWEST)
    top = jnp.maximum(top_ref[...], part_top)
    own = jnp.exp2((top_ref[...] - top) * FACTOR)
    weight = jnp.where(part_total > 0.0, jnp.exp2((part_top - top) * FACTOR) * part_total, 0.0)
    inverse = 1.0 / (total_ref[...] * own + weight)
    own = own * inverse
    weight = weight * inverse
    rows = own_ref.shape[0]
    heads = own_ref.shape[1] // HD
    for i, out_ref in ((1, mate_ref), (0, own_ref)):
        for h in range(heads):
            at = slice((i * heads + h) * rows, (i * heads + h + 1) * rows)
            mixed = acc_ref[:, at] * own[:, at] + part[:, at] * weight[:, at]
            out_ref[:, h * HD : (h + 1) * HD] = jnp.transpose(mixed).astype(jnp.bfloat16)


def place_kernel(at_ref, own_ref, mate_ref, pages_ref, out_ref, pool_ref):
    group = lax.rem(lax.div(at_ref[1], 2), 2)
    width = own_ref.shape[1]
    out_ref[:, pl.ds(pl.multiple_of(group * width, HD), width)] = own_ref[...]
    out_ref[:, pl.ds(pl.multiple_of((1 - group) * width, HD), width)] = mate_ref[...]
    slots = pool_ref.shape[0]
    for i in range(pages_ref.shape[0] // slots):
        pool_ref[:, :, :, i * HD : (i + 1) * HD] = pages_ref[i * slots : (i + 1) * slots]


SMEM = pl.BlockSpec(memory_space=pltpu.SMEM)
VMEM = pl.BlockSpec(memory_space=pltpu.VMEM)
ANY = pl.BlockSpec(memory_space=pl.ANY)
MIB = 1 << 20


def call(kernel, out_shape, in_specs, name, flops, scratch=(), vmem=40 * MIB):
    several = isinstance(out_shape, tuple)
    return pl.pallas_call(
        kernel,
        out_shape=out_shape,
        in_specs=in_specs,
        out_specs=(VMEM,) * len(out_shape) if several else VMEM,
        scratch_shapes=scratch,
        compiler_params=pltpu.CompilerParams(vmem_limit_bytes=vmem),
        cost_estimate=pl.CostEstimate(flops=flops, bytes_accessed=3 << 20, transcendentals=0),
        name=name,
    )


def body(queries, keys, values, doc_lengths, page_table):
    rows = queries.shape[0]
    n_head = lax.axis_size("head")
    n_pb = lax.axis_size("pb")
    n_kv = lax.axis_size("kv")
    chips = n_kv // 2
    columns = queries.shape[1]
    lanes = columns // HD * rows // 2
    n_slots = rows // PAGE * 2
    shape = jax.ShapeDtypeStruct
    at = jnp.stack([lax.axis_index("pb"), lax.axis_index("kv"), n_pb, n_kv, n_head]).astype(jnp.int32)
    to_mate = [(i, i ^ 2) for i in range(n_kv)]

    sent = call(
        spread_kernel, shape((chips, rows, 2 * HD), jnp.bfloat16), [ANY] * 2, "spread_keys", 1 << 10,
        [pltpu.VMEM((rows, 2 * keys.shape[1]), jnp.bfloat16), pltpu.SemaphoreType.DMA((2,))], 60 * MIB,
    )(keys, values)
    ring = [[2 * i + core for i in range(chips)] for core in range(2)]
    mine = lax.all_to_all(sent, "kv", 0, 0, tiled=True, axis_index_groups=ring)
    half = shape((HD, lanes), jnp.bfloat16)
    keep, give = call(turn_kernel, (half, half), [SMEM, VMEM], "turn_queries", 1 << 20)(at, queries)
    mate = lax.ppermute(give, "kv", to_mate)
    later = lax.ppermute(keep, "pb", [(i + 1, i) for i in range(n_pb - 1)])
    steps = [((z + 1) * n_kv + (i ^ 2), z * n_kv + i) for z in range(n_pb - 1) for i in range(n_kv)]
    later_mate = lax.ppermute(give, ("pb", "kv"), steps)
    mine, mate, later, later_mate = lax.optimization_barrier((mine, mate, later, later_mate))
    other = lax.ppermute(mine, "kv", [(i, i ^ 1) for i in range(n_kv)])

    flops = 4 * columns * rows * n_kv * rows
    state = [(HD, 2 * lanes), (1, 2 * lanes), (1, 2 * lanes)]
    kept = pltpu.VMEM((chips // SPAN, 2, 2 * rows * SPAN, lanes), jnp.float32)
    scanned = [SMEM, SMEM, VMEM, VMEM, VMEM, VMEM]
    part = call(
        later_kernel, shape((HD + STAT_ROWS, 2 * lanes), jnp.bfloat16), scanned, "later_rows", flops,
        [pltpu.VMEM(one, jnp.float32) for one in state] + [kept],
    )(at, doc_lengths, later, later_mate, mine, other)
    back = lax.ppermute(part, "pb", [(i, i + 1) for i in range(n_pb - 1)])
    pages = call(
        pick_kernel, shape((n_slots, 2, PAGE, HD), jnp.bfloat16), [SMEM, SMEM, VMEM, VMEM], "pick_pages", 1 << 20
    )(at, page_table, mine, other)
    sharing = [
        [head * n_kv + (2 * pair + chip) * 2 + core for head in range(n_head) for chip in range(2)]
        for pair in range(chips // 2)
        for core in range(2)
    ]
    arrived = lax.all_to_all(pages, ("head", "kv"), 0, 0, tiled=True, axis_index_groups=sharing)
    own = call(
        own_kernel, tuple(shape(one, jnp.float32) for one in state), scanned, "own_row", flops, [kept]
    )(at, doc_lengths, keep, mate, mine, other)
    out = shape((rows, columns // 2), jnp.bfloat16)
    own_out, mate_out = call(join_kernel, (out, out), [VMEM] * 4, "join_rows", 1 << 20)(*own, back)
    mate_out = lax.ppermute(mate_out, "kv", to_mate)
    pool = shape((n_slots // (2 * n_head), 2, PAGE, 2 * n_head * HD), jnp.bfloat16)
    return call(
        place_kernel, (shape((rows, columns), jnp.bfloat16), pool), [SMEM] + [VMEM] * 3, "place", 1 << 10
    )(at, own_out, mate_out, arrived)


def solution(mesh):
    in_specs = (P(("pb", "kv"), "head"), P(("pb", "kv"), "head"), P(("pb", "kv"), "head"), P(), P())
    out_specs = (P(("pb", "kv"), "head"), P(("head", "pb", "kv"), None, None, None))
    return jax.shard_map(body, mesh=mesh, in_specs=in_specs, out_specs=out_specs, check_vma=False)
```

```python
import functools
import math

import jax
import jax.numpy as jnp
from jax import lax
from jax.experimental import pallas as pl
from jax.experimental.pallas import tpu as pltpu
from jax.sharding import PartitionSpec as P

HD = 128
PAGE = 16
SPAN = 2
LOWEST = -1e30
STAT_ROWS = 16
LONG = 10**11
FACTOR = HD**-0.5 * math.log2(math.e)


def doc_start(lengths_ref, position):
    bound = jnp.int32(0)
    start = jnp.zeros_like(position)
    for i in range(lengths_ref.shape[0]):
        bound = bound + lengths_ref[i]
        start = jnp.where(bound <= position, bound, start)
    return start


def spread_kernel(keys_ref, values_ref, out_ref, keys, values, both, sems):
    loads = [
        pltpu.make_async_copy(keys_ref, keys, sems.at[0]),
        pltpu.make_async_copy(values_ref, values, sems.at[1]),
    ]
    for copy in loads:
        copy.start()
    for copy in loads:
        copy.wait()
    copies = []
    for group in range(2):
        cols = slice(group * HD, (group + 1) * HD)
        both[group, :, 0:HD] = keys[:, cols]
        both[group, :, HD : 2 * HD] = values[:, cols]
        for chip in range(group, out_ref.shape[0], 2):
            copies.append(pltpu.make_async_copy(both.at[group], out_ref.at[chip], sems.at[2 + chip]))
            copies[-1].start()
    for copy in copies:
        copy.wait()


def turn_kernel(q_ref, keep_ref, give_ref):
    group = lax.rem(lax.div(lax.axis_index("kv"), 2), 2)
    rows = q_ref.shape[0]
    heads = keep_ref.shape[1] // rows
    for out_ref, one in ((keep_ref, group), (give_ref, 1 - group)):
        for h in range(heads):
            cols = pl.ds(pl.multiple_of((one * heads + h) * HD, HD), HD)
            out_ref[:, h * rows : (h + 1) * rows] = jnp.transpose(q_ref[:, cols])


def scan_keys(lengths_ref, q_refs, mine_ref, other_ref, q_bases, k_base, core, acc, top, total, kept, SPAN=SPAN):
    rows = mine_ref.shape[1]
    lanes = q_refs[0].shape[1]
    heads = lanes // rows
    tile = 2 * rows * SPAN
    count = mine_ref.shape[0] // SPAN
    acc[...] = jnp.zeros_like(acc)
    top[...] = jnp.full_like(top, LOWEST)
    total[...] = jnp.zeros_like(total)
    q_low = functools.reduce(jnp.minimum, q_bases)
    q_high = functools.reduce(jnp.maximum, q_bases) + rows - 1
    first_start = doc_start(lengths_ref, q_low)
    last_start = doc_start(lengths_ref, q_high)
    q_pos = [base + lax.broadcasted_iota(jnp.int32, (1, rows), 1) for base in q_bases]
    q_start = [doc_start(lengths_ref, one) for one in q_pos]
    low_tile = jnp.clip(lax.div(first_start - k_base, tile), 0, count)
    high_tile = jnp.clip(lax.div(q_high - k_base, tile) + 1, 0, count)

    def columns(at, cols):
        parts = []
        for chip in range(SPAN):
            parts += [mine_ref[at * SPAN + chip, :, cols], other_ref[at * SPAN + chip, :, cols]]
        return jnp.concatenate(parts, axis=0)

    def score(at, masked):
        keys = columns(at, slice(0, HD))
        if masked:
            row = lax.broadcasted_iota(jnp.int32, (2 * rows, rows), 0)
            k_pos = k_base + at * tile + jnp.where(row < rows, row + core * rows, row - core * rows)
            k_pos = jnp.concatenate([k_pos + chip * 2 * rows for chip in range(SPAN)], axis=0)
        for i, q_ref in enumerate(q_refs):
            where = slice(i * lanes, (i + 1) * lanes)
            scores = jnp.dot(keys, q_ref[...], preferred_element_type=jnp.float32)
            if masked:
                seen = (k_pos <= q_pos[i]) & (k_pos >= q_start[i])
                scores = jnp.where(jnp.concatenate([seen] * heads, axis=1), scores, LOWEST)
            kept[at, i] = scores
            top[:, where] = jnp.maximum(top[:, where], jnp.max(scores, axis=0, keepdims=True))

    def first_pass(at, carry):
        low = k_base + at * tile
        whole = (low + tile - 1 <= q_low) & (low >= last_start)

        @pl.when(whole)
        def _():
            score(at, False)

        @pl.when(jnp.logical_not(whole))
        def _():
            score(at, True)

        return carry

    def second_pass(at, carry):
        values = columns(at, slice(HD, 2 * HD))
        for i in range(len(q_refs)):
            where = slice(i * lanes, (i + 1) * lanes)
            peak = jnp.maximum(top[:, where], 0.1 * LOWEST) * FACTOR
            weights = jnp.exp2(kept[at, i] * FACTOR - peak)
            total[:, where] = total[:, where] + jnp.sum(weights, axis=0, keepdims=True)
            acc[:, where] = acc[:, where] + lax.dot_general(
                values, weights.astype(jnp.bfloat16), (((0,), (0,)), ((), ())), preferred_element_type=jnp.float32
            )
        return carry

    lax.fori_loop(low_tile, high_tile, first_pass, 0)
    lax.fori_loop(low_tile, high_tile, second_pass, 0)


def split_three(value):
    high = value.astype(jnp.bfloat16)
    rest = value - high.astype(jnp.float32)
    middle = rest.astype(jnp.bfloat16)
    low = (rest - middle.astype(jnp.float32)).astype(jnp.bfloat16)
    return [high, middle, low]


def bases(rows, later):
    pb, kv = lax.axis_index("pb"), lax.axis_index("kv")
    row_tokens = lax.axis_size("kv") * rows
    chip = lax.div(kv, 2)
    mate = (chip + 1 - 2 * lax.rem(chip, 2)) * 2 + lax.rem(kv, 2)
    q_row = (pb + later) * row_tokens
    return (q_row + kv * rows, q_row + mate * rows), pb * row_tokens, lax.rem(kv, 2)


def pick_pages(table_ref, mine_ref, other_ref, pages_ref):
    pb, kv = lax.axis_index("pb"), lax.axis_index("kv")
    n_head, n_pb, n_kv = lax.axis_size("head"), lax.axis_size("pb"), lax.axis_size("kv")
    core = lax.rem(kv, 2)
    rows = mine_ref.shape[1]
    n_slots = pages_ref.shape[0]
    row_pages = n_kv * rows // PAGE
    slot_rows = row_pages // n_head
    per = n_slots // 8
    first_chip = lax.div(kv, 4) * 2
    for i in range(n_slots):
        head, chip, which = i // (2 * per), i // per % 2, i % per
        slot = head * (n_pb * slot_rows) + pb * slot_rows + ((first_chip + chip) * 2 + core) * per + which
        page = table_ref[slot] - pb * row_pages
        block_pages = rows // PAGE
        block = lax.div(page, block_pages)
        held = lax.div(block, 2)
        row = pl.multiple_of(lax.rem(page, block_pages) * PAGE, PAGE)
        own = lax.rem(block, 2) == core
        for half in range(2):
            cols = slice(half * HD, (half + 1) * HD)
            pages_ref[i, half] = jnp.where(
                own, mine_ref[held, pl.ds(row, PAGE), cols], other_ref[held, pl.ds(row, PAGE), cols]
            )


def later_kernel(
    lengths_ref, table_ref, q_ref, mate_ref, mine_ref, other_ref, part_ref, pages_ref, acc, top, total, kept
):
    pick_pages(table_ref, mine_ref, other_ref, pages_ref)
    q_bases, k_base, core = bases(mine_ref.shape[1], 1)
    scan_keys(lengths_ref, (q_ref, mate_ref), mine_ref, other_ref, q_bases, k_base, core, acc, top, total, kept)
    part_ref[0:HD, :] = (acc[...] / jnp.maximum(total[...], 1e-30)).astype(jnp.bfloat16)
    stats = split_three(top[...]) + split_three(total[...])
    stats.append(jnp.zeros((STAT_ROWS - len(stats), acc.shape[1]), jnp.bfloat16))
    part_ref[HD : HD + STAT_ROWS, :] = jnp.concatenate(stats, axis=0)


def join(acc, top, total, part_ref, which, out_ref):
    rows = out_ref.shape[0]
    lanes = acc.shape[1]
    at = slice(which * lanes, (which + 1) * lanes)
    part = part_ref[0:HD, at].astype(jnp.float32)
    stats = part_ref[HD : HD + STAT_ROWS, at].astype(jnp.float32)
    part_total = stats[3:4] + stats[4:5] + stats[5:6]
    part_top = jnp.where(part_total > 0.0, stats[0:1] + stats[1:2] + stats[2:3], LOWEST)
    peak = jnp.maximum(top[...], part_top)
    own = jnp.exp2((top[...] - peak) * FACTOR)
    weight = jnp.where(part_total > 0.0, jnp.exp2((part_top - peak) * FACTOR) * part_total, 0.0)
    inverse = 1.0 / (total[...] * own + weight)
    mixed = acc[...] * (own * inverse) + part * (weight * inverse)
    for h in range(lanes // rows):
        out_ref[:, h * HD : (h + 1) * HD] = jnp.transpose(mixed[:, h * rows : (h + 1) * rows]).astype(jnp.bfloat16)


def mate_kernel(lengths_ref, q_ref, mine_ref, other_ref, acc, top, total, kept):
    q_bases, k_base, core = bases(mine_ref.shape[1], 0)
    scan_keys(lengths_ref, (q_ref,), mine_ref, other_ref, q_bases[1:], k_base, core, acc, top, total, kept)


def mate_join_kernel(acc, top, total, part_ref, out_ref):
    join(acc, top, total, part_ref, 1, out_ref)


def own_kernel(lengths_ref, q_ref, mine_ref, other_ref, part_ref, out_ref, acc, top, total, kept):
    q_bases, k_base, core = bases(mine_ref.shape[1], 0)
    scan_keys(lengths_ref, (q_ref,), mine_ref, other_ref, q_bases[:1], k_base, core, acc, top, total, kept)
    join(acc, top, total, part_ref, 0, out_ref)


def place_kernel(own_ref, mate_ref, pages_ref, out_ref, pool_ref):
    group = lax.rem(lax.div(lax.axis_index("kv"), 2), 2)
    width = own_ref.shape[1]
    out_ref[:, pl.ds(pl.multiple_of(group * width, HD), width)] = own_ref[...]
    out_ref[:, pl.ds(pl.multiple_of((1 - group) * width, HD), width)] = mate_ref[...]
    slots = pool_ref.shape[0]
    for i in range(pages_ref.shape[0] // slots):
        pool_ref[:, :, :, i * HD : (i + 1) * HD] = pages_ref[i * slots : (i + 1) * slots]


SMEM = pl.BlockSpec(memory_space=pltpu.SMEM)
VMEM = pl.BlockSpec(memory_space=pltpu.VMEM)
ANY = pl.BlockSpec(memory_space=pl.ANY)
MIB = 1 << 20


def call(kernel, out_shape, in_specs, name, flops, scratch=(), vmem=40 * MIB, out=None):
    several = isinstance(out_shape, tuple)
    return pl.pallas_call(
        kernel,
        out_shape=out_shape,
        in_specs=in_specs,
        out_specs=out or ((VMEM,) * len(out_shape) if several else VMEM),
        scratch_shapes=scratch,
        compiler_params=pltpu.CompilerParams(vmem_limit_bytes=vmem),
        cost_estimate=pl.CostEstimate(flops=flops, bytes_accessed=3 << 20, transcendentals=0),
        name=name,
    )


def body(queries, keys, values, doc_lengths, page_table):
    rows = queries.shape[0]
    n_head = lax.axis_size("head")
    n_pb = lax.axis_size("pb")
    n_kv = lax.axis_size("kv")
    chips = n_kv // 2
    columns = queries.shape[1]
    lanes = columns // HD * rows // 2
    n_slots = rows // PAGE * 2
    shape = jax.ShapeDtypeStruct
    to_mate = [(i, i ^ 2) for i in range(n_kv)]

    local = [pltpu.VMEM(keys.shape, jnp.bfloat16)] * 2 + [pltpu.VMEM((2, rows, 2 * HD), jnp.bfloat16)]
    sent = call(
        spread_kernel, shape((chips, rows, 2 * HD), jnp.bfloat16), [ANY] * 2, "spread_keys", 1 << 10,
        local + [pltpu.SemaphoreType.DMA((2 + chips,))], 60 * MIB, ANY,
    )(keys, values)
    ring = [[2 * i + core for i in range(chips)] for core in range(2)]
    mine = lax.all_to_all(sent, "kv", 0, 0, tiled=True, axis_index_groups=ring)
    half = shape((HD, lanes), jnp.bfloat16)
    keep, give = call(turn_kernel, (half, half), [VMEM], "turn_queries", 1 << 20)(queries)
    mate = lax.ppermute(give, "kv", to_mate)
    later = lax.ppermute(keep, "pb", [(i + 1, i) for i in range(n_pb - 1)])
    steps = [((z + 1) * n_kv + (i ^ 2), z * n_kv + i) for z in range(n_pb - 1) for i in range(n_kv)]
    later_mate = lax.ppermute(give, ("pb", "kv"), steps)
    mine, later, later_mate = lax.optimization_barrier((mine, later, later_mate))
    other = lax.ppermute(mine, "kv", [(i, i ^ 1) for i in range(n_kv)])

    def scratch(sets):
        state = [(HD, sets * lanes), (1, sets * lanes), (1, sets * lanes)]
        kept = pltpu.VMEM((chips // SPAN, sets, 2 * rows * SPAN, lanes), jnp.float32)
        return [shape(one, jnp.float32) for one in state], [pltpu.VMEM(one, jnp.float32) for one in state], kept

    _, state, kept = scratch(2)
    part, pages = call(
        later_kernel,
        (shape((HD + STAT_ROWS, 2 * lanes), jnp.bfloat16), shape((n_slots, 2, PAGE, HD), jnp.bfloat16)),
        [SMEM] * 2 + [VMEM] * 4, "later_rows", LONG, state + [kept],
    )(doc_lengths, page_table, later, later_mate, mine, other)
    back = lax.ppermute(part, "pb", [(i, i + 1) for i in range(n_pb - 1)])
    sharing = [
        [head * n_kv + (2 * pair + chip) * 2 + core for head in range(n_head) for chip in range(2)]
        for pair in range(chips // 2)
        for core in range(2)
    ]
    arrived = lax.all_to_all(pages, ("head", "kv"), 0, 0, tiled=True, axis_index_groups=sharing)
    shapes, state, kept = scratch(1)
    out = shape((rows, columns // 2), jnp.bfloat16)
    mate_own = call(mate_kernel, tuple(shapes), [SMEM] + [VMEM] * 3, "mate_row", LONG, [kept])(
        doc_lengths, mate, mine, other
    )
    mate_out = call(mate_join_kernel, out, [VMEM] * 4, "mate_join", 1 << 20)(*mate_own, back)
    mate_out = lax.ppermute(mate_out, "kv", to_mate)
    own_out = call(own_kernel, out, [SMEM] + [VMEM] * 4, "own_row", 1 << 30, state + [kept])(
        doc_lengths, keep, mine, other, back
    )
    pool = shape((n_slots // (2 * n_head), 2, PAGE, 2 * n_head * HD), jnp.bfloat16)
    return call(
        place_kernel, (shape((rows, columns), jnp.bfloat16), pool), [VMEM] * 3, "place", 1 << 10
    )(own_out, mate_out, arrived)


def solution(mesh):
    in_specs = (P(("pb", "kv"), "head"), P(("pb", "kv"), "head"), P(("pb", "kv"), "head"), P(), P())
    out_specs = (P(("pb", "kv"), "head"), P(("head", "pb", "kv"), None, None, None))
    return jax.shard_map(body, mesh=mesh, in_specs=in_specs, out_specs=out_specs, check_vma=False)
```

```python
import functools
import math

import jax
import jax.numpy as jnp
from jax import lax
from jax.experimental import pallas as pl
from jax.experimental.pallas import tpu as pltpu
from jax.sharding import PartitionSpec as P

HD = 128
PAGE = 16
SPAN = 2
LOWEST = -1e30
STAT_ROWS = 16
PLAN_PAGES = 7
LONG = 10**11
FACTOR = HD**-0.5 * math.log2(math.e)


def doc_start(lengths_ref, position):
    bound = jnp.int32(0)
    start = jnp.zeros_like(position)
    for i in range(lengths_ref.shape[0]):
        bound = bound + lengths_ref[i]
        start = jnp.where(bound <= position, bound, start)
    return start


def spread_kernel(keys_ref, values_ref, out_ref, keys, values, both, sems):
    loads = [
        pltpu.make_async_copy(keys_ref, keys, sems.at[0]),
        pltpu.make_async_copy(values_ref, values, sems.at[1]),
    ]
    for copy in loads:
        copy.start()
    for copy in loads:
        copy.wait()
    copies = []
    for group in range(2):
        cols = slice(group * HD, (group + 1) * HD)
        both[group, :, 0:HD] = keys[:, cols]
        both[group, :, HD : 2 * HD] = values[:, cols]
        for chip in range(group, out_ref.shape[0], 2):
            copies.append(pltpu.make_async_copy(both.at[group], out_ref.at[chip], sems.at[2 + chip]))
            copies[-1].start()
    for copy in copies:
        copy.wait()


def bases(rows, later):
    pb, kv = lax.axis_index("pb"), lax.axis_index("kv")
    row_tokens = lax.axis_size("kv") * rows
    chip = lax.div(kv, 2)
    mate = (chip + 1 - 2 * lax.rem(chip, 2)) * 2 + lax.rem(kv, 2)
    q_row = (pb + later) * row_tokens
    return (q_row + kv * rows, q_row + mate * rows), pb * row_tokens, lax.rem(kv, 2)


def page_codes(table_ref, rows, n_slots):
    pb, kv = lax.axis_index("pb"), lax.axis_index("kv")
    n_head, n_pb, n_kv = lax.axis_size("head"), lax.axis_size("pb"), lax.axis_size("kv")
    row_pages = n_kv * rows // PAGE
    slot_rows = row_pages // n_head
    per = n_slots // (2 * n_head)
    first_chip = lax.div(kv, 4) * 2
    block_pages = rows // PAGE
    for i in range(n_slots):
        head, chip, which = i // (2 * per), i // per % 2, i % per
        slot = head * (n_pb * slot_rows) + pb * slot_rows + ((first_chip + chip) * 2 + lax.rem(kv, 2)) * per + which
        page = table_ref[slot] - pb * row_pages
        block = lax.div(page, block_pages)
        row = lax.div(block, 2) * rows + lax.rem(page, block_pages) * PAGE
        yield 2 * row + (lax.rem(block, 2) == lax.rem(kv, 2)).astype(jnp.int32)


def turn_kernel(lengths_ref, table_ref, q_ref, keep_ref, give_ref, plan_ref, *, n_slots):
    group = lax.rem(lax.div(lax.axis_index("kv"), 2), 2)
    rows = q_ref.shape[0]
    heads = keep_ref.shape[1] // rows
    for out_ref, one in ((keep_ref, group), (give_ref, 1 - group)):
        for h in range(heads):
            cols = pl.ds(pl.multiple_of((one * heads + h) * HD, HD), HD)
            out_ref[:, h * rows : (h + 1) * rows] = jnp.transpose(q_ref[:, cols])
    lane = lax.broadcasted_iota(jnp.int32, (1, rows), 1)
    plan = [doc_start(lengths_ref, base + lane) for later in range(2) for base in bases(rows, later)[0]]
    pages = jnp.zeros((1, rows), jnp.int32)
    for i, code in enumerate(page_codes(table_ref, rows, n_slots)):
        pages = jnp.where(lane == i, code, pages)
    plan += [pages] * (plan_ref.shape[0] - len(plan))
    plan_ref[...] = jnp.concatenate(plan, axis=0)


def scan_keys(plan_ref, sets, q_refs, mine_ref, other_ref, q_bases, k_base, core, acc, top, total, kept):
    rows = mine_ref.shape[1]
    lanes = q_refs[0].shape[1]
    heads = lanes // rows
    tile = 2 * rows * SPAN
    count = mine_ref.shape[0] // SPAN
    acc[...] = jnp.zeros_like(acc)
    top[...] = jnp.full_like(top, LOWEST)
    total[...] = jnp.zeros_like(total)
    q_low = functools.reduce(jnp.minimum, q_bases)
    q_high = functools.reduce(jnp.maximum, q_bases) + rows - 1
    first_start = functools.reduce(jnp.minimum, [plan_ref[i, 0] for i in sets])
    last_start = functools.reduce(jnp.maximum, [plan_ref[i, rows - 1] for i in sets])
    q_pos = [base + lax.broadcasted_iota(jnp.int32, (1, rows), 1) for base in q_bases]
    q_start = [plan_ref[i : i + 1, :] for i in sets]
    low_tile = jnp.clip(lax.div(first_start - k_base, tile), 0, count)
    high_tile = jnp.clip(lax.div(q_high - k_base, tile) + 1, 0, count)

    def columns(at, cols):
        parts = []
        for chip in range(SPAN):
            parts += [mine_ref[at * SPAN + chip, :, cols], other_ref[at * SPAN + chip, :, cols]]
        return jnp.concatenate(parts, axis=0)

    def score(at, masked):
        keys = columns(at, slice(0, HD))
        if masked:
            row = lax.broadcasted_iota(jnp.int32, (2 * rows, rows), 0)
            k_pos = k_base + at * tile + jnp.where(row < rows, row + core * rows, row - core * rows)
            k_pos = jnp.concatenate([k_pos + chip * 2 * rows for chip in range(SPAN)], axis=0)
        for i, q_ref in enumerate(q_refs):
            where = slice(i * lanes, (i + 1) * lanes)
            scores = jnp.dot(keys, q_ref[...], preferred_element_type=jnp.float32)
            if masked:
                seen = (k_pos <= q_pos[i]) & (k_pos >= q_start[i])
                scores = jnp.where(jnp.concatenate([seen] * heads, axis=1), scores, LOWEST)
            kept[at, i] = scores
            top[:, where] = jnp.maximum(top[:, where], jnp.max(scores, axis=0, keepdims=True))

    def first_pass(at, carry):
        low = k_base + at * tile
        whole = (low + tile - 1 <= q_low) & (low >= last_start)

        @pl.when(whole)
        def _():
            score(at, False)

        @pl.when(jnp.logical_not(whole))
        def _():
            score(at, True)

        return carry

    def second_pass(at, carry):
        values = columns(at, slice(HD, 2 * HD))
        for i in range(len(q_refs)):
            where = slice(i * lanes, (i + 1) * lanes)
            peak = jnp.maximum(top[:, where], 0.1 * LOWEST) * FACTOR
            weights = jnp.exp2(kept[at, i] * FACTOR - peak)
            total[:, where] = total[:, where] + jnp.sum(weights, axis=0, keepdims=True)
            acc[:, where] = acc[:, where] + lax.dot_general(
                values, weights.astype(jnp.bfloat16), (((0,), (0,)), ((), ())), preferred_element_type=jnp.float32
            )
        return carry

    lax.fori_loop(low_tile, high_tile, first_pass, 0)
    lax.fori_loop(low_tile, high_tile, second_pass, 0)


def split_three(value):
    high = value.astype(jnp.bfloat16)
    rest = value - high.astype(jnp.float32)
    middle = rest.astype(jnp.bfloat16)
    low = (rest - middle.astype(jnp.float32)).astype(jnp.bfloat16)
    return [high, middle, low]


def pick_pages(plan_ref, mine_ref, other_ref, pages_ref):
    rows = mine_ref.shape[1]
    for i in range(pages_ref.shape[0]):
        code = plan_ref[PLAN_PAGES, i]
        own = lax.rem(code, 2) == 1
        place = lax.div(code, 2)
        chip = lax.div(place, rows)
        row = pl.multiple_of(lax.rem(place, rows), PAGE)
        for half in range(2):
            cols = slice(half * HD, (half + 1) * HD)
            pages_ref[i, half] = jnp.where(
                own, mine_ref[chip, pl.ds(row, PAGE), cols], other_ref[chip, pl.ds(row, PAGE), cols]
            )


def later_kernel(
    plan_ref, q_ref, mate_ref, mine_ref, other_ref, part_ref, pages_ref, acc, top, total, kept, picked, sem
):
    pick_pages(plan_ref, mine_ref, other_ref, picked)
    leave = pltpu.make_async_copy(picked, pages_ref, sem)
    leave.start()
    q_bases, k_base, core = bases(mine_ref.shape[1], 1)
    scan_keys(plan_ref, (2, 3), (q_ref, mate_ref), mine_ref, other_ref, q_bases, k_base, core, acc, top, total, kept)
    part_ref[0:HD, :] = (acc[...] / jnp.maximum(total[...], 1e-30)).astype(jnp.bfloat16)
    stats = split_three(top[...]) + split_three(total[...])
    stats.append(jnp.zeros((STAT_ROWS - len(stats), acc.shape[1]), jnp.bfloat16))
    part_ref[HD : HD + STAT_ROWS, :] = jnp.concatenate(stats, axis=0)
    leave.wait()


def join(acc, top, total, part_ref, which, out_ref):
    rows = out_ref.shape[0]
    lanes = acc.shape[1]
    at = slice(which * lanes, (which + 1) * lanes)
    part = part_ref[0:HD, at].astype(jnp.float32)
    stats = part_ref[HD : HD + STAT_ROWS, at].astype(jnp.float32)
    part_total = stats[3:4] + stats[4:5] + stats[5:6]
    part_top = jnp.where(part_total > 0.0, stats[0:1] + stats[1:2] + stats[2:3], LOWEST)
    peak = jnp.maximum(top[...], part_top)
    own = jnp.exp2((top[...] - peak) * FACTOR)
    weight = jnp.where(part_total > 0.0, jnp.exp2((part_top - peak) * FACTOR) * part_total, 0.0)
    inverse = 1.0 / (total[...] * own + weight)
    mixed = acc[...] * (own * inverse) + part * (weight * inverse)
    for h in range(lanes // rows):
        out_ref[:, h * HD : (h + 1) * HD] = jnp.transpose(mixed[:, h * rows : (h + 1) * rows]).astype(jnp.bfloat16)


def mate_kernel(plan_ref, q_ref, mine_ref, other_ref, acc, top, total, kept):
    q_bases, k_base, core = bases(mine_ref.shape[1], 0)
    scan_keys(plan_ref, (1,), (q_ref,), mine_ref, other_ref, q_bases[1:], k_base, core, acc, top, total, kept)


def mate_join_kernel(acc, top, total, part_ref, out_ref):
    join(acc, top, total, part_ref, 1, out_ref)


def own_kernel(plan_ref, q_ref, mine_ref, other_ref, part_ref, out_ref, acc, top, total, kept):
    q_bases, k_base, core = bases(mine_ref.shape[1], 0)
    scan_keys(plan_ref, (0,), (q_ref,), mine_ref, other_ref, q_bases[:1], k_base, core, acc, top, total, kept)
    join(acc, top, total, part_ref, 0, out_ref)


def place_kernel(own_ref, mate_ref, pages_ref, out_ref, pool_ref):
    group = lax.rem(lax.div(lax.axis_index("kv"), 2), 2)
    width = own_ref.shape[1]
    out_ref[:, pl.ds(pl.multiple_of(group * width, HD), width)] = own_ref[...]
    out_ref[:, pl.ds(pl.multiple_of((1 - group) * width, HD), width)] = mate_ref[...]
    slots = pool_ref.shape[0]
    for i in range(pages_ref.shape[0] // slots):
        pool_ref[:, :, :, i * HD : (i + 1) * HD] = pages_ref[i * slots : (i + 1) * slots]


SMEM = pl.BlockSpec(memory_space=pltpu.SMEM)
VMEM = pl.BlockSpec(memory_space=pltpu.VMEM)
ANY = pl.BlockSpec(memory_space=pl.ANY)
MIB = 1 << 20


def call(kernel, out_shape, in_specs, name, flops, scratch=(), vmem=40 * MIB, out=None):
    several = isinstance(out_shape, tuple)
    return pl.pallas_call(
        kernel,
        out_shape=out_shape,
        in_specs=in_specs,
        out_specs=out or ((VMEM,) * len(out_shape) if several else VMEM),
        scratch_shapes=scratch,
        compiler_params=pltpu.CompilerParams(vmem_limit_bytes=vmem),
        cost_estimate=pl.CostEstimate(flops=flops, bytes_accessed=3 << 20, transcendentals=0),
        name=name,
    )


def body(queries, keys, values, doc_lengths, page_table):
    rows = queries.shape[0]
    n_head = lax.axis_size("head")
    n_pb = lax.axis_size("pb")
    n_kv = lax.axis_size("kv")
    chips = n_kv // 2
    columns = queries.shape[1]
    lanes = columns // HD * rows // 2
    n_slots = rows // PAGE * 2
    shape = jax.ShapeDtypeStruct
    to_mate = [(i, i ^ 2) for i in range(n_kv)]

    local = [pltpu.VMEM(keys.shape, jnp.bfloat16)] * 2 + [pltpu.VMEM((2, rows, 2 * HD), jnp.bfloat16)]
    sent = call(
        spread_kernel, shape((chips, rows, 2 * HD), jnp.bfloat16), [ANY] * 2, "spread_keys", 1 << 10,
        local + [pltpu.SemaphoreType.DMA((2 + chips,))], 60 * MIB, ANY,
    )(keys, values)
    ring = [[2 * i + core for i in range(chips)] for core in range(2)]
    mine = lax.all_to_all(sent, "kv", 0, 0, tiled=True, axis_index_groups=ring)
    half = shape((HD, lanes), jnp.bfloat16)
    plan = shape((PLAN_PAGES + 1, rows), jnp.int32)
    turn = functools.partial(turn_kernel, n_slots=n_slots)
    keep, give, plan = call(turn, (half, half, plan), [SMEM, SMEM, VMEM], "turn_queries", 1 << 20)(
        doc_lengths, page_table, queries
    )
    mate = lax.ppermute(give, "kv", to_mate)
    later = lax.ppermute(keep, "pb", [(i + 1, i) for i in range(n_pb - 1)])
    steps = [((z + 1) * n_kv + (i ^ 2), z * n_kv + i) for z in range(n_pb - 1) for i in range(n_kv)]
    later_mate = lax.ppermute(give, ("pb", "kv"), steps)
    mine, later, later_mate = lax.optimization_barrier((mine, later, later_mate))
    other = lax.ppermute(mine, "kv", [(i, i ^ 1) for i in range(n_kv)])

    def scratch(sets):
        state = [(HD, sets * lanes), (1, sets * lanes), (1, sets * lanes)]
        kept = pltpu.VMEM((chips // SPAN, sets, 2 * rows * SPAN, lanes), jnp.float32)
        return [shape(one, jnp.float32) for one in state], [pltpu.VMEM(one, jnp.float32) for one in state], kept

    _, state, kept = scratch(2)
    part, pages = call(
        later_kernel,
        (shape((HD + STAT_ROWS, 2 * lanes), jnp.bfloat16), shape((n_slots, 2, PAGE, HD), jnp.bfloat16)),
        [VMEM] * 5, "later_rows", LONG,
        state + [kept, pltpu.VMEM((n_slots, 2, PAGE, HD), jnp.bfloat16), pltpu.SemaphoreType.DMA], out=(VMEM, ANY),
    )(plan, later, later_mate, mine, other)
    back = lax.ppermute(part, "pb", [(i, i + 1) for i in range(n_pb - 1)])
    sharing = [
        [head * n_kv + (2 * pair + chip) * 2 + core for head in range(n_head) for chip in range(2)]
        for pair in range(chips // 2)
        for core in range(2)
    ]
    arrived = lax.all_to_all(pages, ("head", "kv"), 0, 0, tiled=True, axis_index_groups=sharing)
    shapes, state, kept = scratch(1)
    out = shape((rows, columns // 2), jnp.bfloat16)
    mate_own = call(mate_kernel, tuple(shapes), [VMEM] * 4, "mate_row", LONG, [kept])(
        plan, mate, mine, other
    )
    mate_out = call(mate_join_kernel, out, [VMEM] * 4, "mate_join", 1 << 20)(*mate_own, back)
    mate_out = lax.ppermute(mate_out, "kv", to_mate)
    own_out = call(own_kernel, out, [VMEM] * 5, "own_row", 1 << 30, state + [kept])(
        plan, keep, mine, other, back
    )
    pool = shape((n_slots // (2 * n_head), 2, PAGE, 2 * n_head * HD), jnp.bfloat16)
    return call(
        place_kernel, (shape((rows, columns), jnp.bfloat16), pool), [VMEM] * 3, "place", 1 << 10
    )(own_out, mate_out, arrived)


def solution(mesh):
    in_specs = (P(("pb", "kv"), "head"), P(("pb", "kv"), "head"), P(("pb", "kv"), "head"), P(), P())
    out_specs = (P(("pb", "kv"), "head"), P(("head", "pb", "kv"), None, None, None))
    return jax.shard_map(body, mesh=mesh, in_specs=in_specs, out_specs=out_specs, check_vma=False)
```

```python
import functools
import math

import jax
import jax.numpy as jnp
from jax import lax
from jax.experimental import pallas as pl
from jax.experimental.pallas import tpu as pltpu
from jax.sharding import PartitionSpec as P

HD = 128
PAGE = 16
SPAN = 2
LOWEST = -1e30
STAT_ROWS = 16
PLAN_PAGES = 7
LONG = 10**11
FACTOR = HD**-0.5 * math.log2(math.e)


def doc_start(lengths_ref, position):
    bound = jnp.int32(0)
    start = jnp.zeros_like(position)
    for i in range(lengths_ref.shape[0]):
        bound = bound + lengths_ref[i]
        start = jnp.where(bound <= position, bound, start)
    return start


def spread_kernel(keys_ref, values_ref, out_ref, keys, values, both, sems):
    loads = [
        pltpu.make_async_copy(keys_ref, keys, sems.at[0]),
        pltpu.make_async_copy(values_ref, values, sems.at[1]),
    ]
    for copy in loads:
        copy.start()
    for copy in loads:
        copy.wait()
    copies = []
    for group in range(2):
        cols = slice(group * HD, (group + 1) * HD)
        both[group, :, 0:HD] = keys[:, cols]
        both[group, :, HD : 2 * HD] = values[:, cols]
        for chip in range(group, out_ref.shape[0], 2):
            copies.append(pltpu.make_async_copy(both.at[group], out_ref.at[chip], sems.at[2 + chip]))
            copies[-1].start()
    for copy in copies:
        copy.wait()


def bases(rows, later):
    pb, kv = lax.axis_index("pb"), lax.axis_index("kv")
    row_tokens = lax.axis_size("kv") * rows
    chip = lax.div(kv, 2)
    mate = (chip + 1 - 2 * lax.rem(chip, 2)) * 2 + lax.rem(kv, 2)
    q_row = (pb + later) * row_tokens
    return (q_row + kv * rows, q_row + mate * rows), pb * row_tokens, lax.rem(kv, 2)


def page_codes(table_ref, rows, n_slots):
    pb, kv = lax.axis_index("pb"), lax.axis_index("kv")
    n_head, n_pb, n_kv = lax.axis_size("head"), lax.axis_size("pb"), lax.axis_size("kv")
    row_pages = n_kv * rows // PAGE
    slot_rows = row_pages // n_head
    per = n_slots // (2 * n_head)
    first_chip = lax.div(kv, 4) * 2
    block_pages = rows // PAGE
    for i in range(n_slots):
        head, chip, which = i // (2 * per), i // per % 2, i % per
        slot = head * (n_pb * slot_rows) + pb * slot_rows + ((first_chip + chip) * 2 + lax.rem(kv, 2)) * per + which
        page = table_ref[slot] - pb * row_pages
        block = lax.div(page, block_pages)
        row = lax.div(block, 2) * rows + lax.rem(page, block_pages) * PAGE
        yield 2 * row + (lax.rem(block, 2) == lax.rem(kv, 2)).astype(jnp.int32)


def turn(q_ref, group, out_ref):
    rows = q_ref.shape[0]
    heads = out_ref.shape[1] // rows
    for h in range(heads):
        cols = pl.ds(pl.multiple_of((group * heads + h) * HD, HD), HD)
        out_ref[:, h * rows : (h + 1) * rows] = jnp.transpose(q_ref[:, cols])


def turn_kernel(lengths_ref, table_ref, q_ref, keep_ref, give_ref, plan_ref, *, n_slots):
    group = lax.rem(lax.div(lax.axis_index("kv"), 2), 2)
    rows = q_ref.shape[0]
    turn(q_ref, group, keep_ref)
    turn(q_ref, 1 - group, give_ref)
    lane = lax.broadcasted_iota(jnp.int32, (1, rows), 1)
    plan = [doc_start(lengths_ref, base + lane) for later in range(2) for base in bases(rows, later)[0]]
    pages = jnp.zeros((1, rows), jnp.int32)
    for i, code in enumerate(page_codes(table_ref, rows, n_slots)):
        pages = jnp.where(lane == i, code, pages)
    plan += [pages] * (plan_ref.shape[0] - len(plan))
    plan_ref[...] = jnp.concatenate(plan, axis=0)


def scan_keys(plan_ref, sets, q_refs, blocks, q_bases, k_base, acc, top, total, kept):
    rows = plan_ref.shape[1]
    lanes = q_refs[0].shape[1]
    heads = lanes // rows
    tile = 2 * rows * SPAN
    count = blocks[0][0].shape[0] // SPAN
    size = len(blocks) * rows * SPAN
    acc[...] = jnp.zeros_like(acc)
    top[...] = jnp.full_like(top, LOWEST)
    total[...] = jnp.zeros_like(total)
    q_low = functools.reduce(jnp.minimum, q_bases)
    q_high = functools.reduce(jnp.maximum, q_bases) + rows - 1
    first_start = functools.reduce(jnp.minimum, [plan_ref[i, 0] for i in sets])
    last_start = functools.reduce(jnp.maximum, [plan_ref[i, rows - 1] for i in sets])
    q_pos = [base + lax.broadcasted_iota(jnp.int32, (1, rows), 1) for base in q_bases]
    q_start = [plan_ref[i : i + 1, :] for i in sets]
    low_tile = jnp.clip(lax.div(first_start - k_base, tile), 0, count)
    high_tile = jnp.clip(lax.div(q_high - k_base, tile) + 1, 0, count)

    def columns(at, cols):
        parts = [ref[at * SPAN + chip, :, cols] for chip in range(SPAN) for ref, _ in blocks]
        return jnp.concatenate(parts, axis=0)

    def score(at, masked, several, carry):
        keys = jnp.concatenate([columns(at + i, slice(0, HD)) for i in range(several)], axis=0)
        if masked:
            row = k_base + at * tile + lax.broadcasted_iota(jnp.int32, (rows, rows), 0)
            k_pos = [row + (2 * chip + core) * rows for chip in range(SPAN) for _, core in blocks]
            k_pos = jnp.concatenate(k_pos, axis=0)
        for i, q_ref in enumerate(q_refs):
            where = slice(i * lanes, (i + 1) * lanes)
            scores = jnp.dot(keys, q_ref[...], preferred_element_type=jnp.float32)
            if masked:
                seen = (k_pos <= q_pos[i]) & (k_pos >= q_start[i])
                scores = jnp.where(jnp.concatenate([seen] * heads, axis=1), scores, LOWEST)
            for more in range(several):
                kept[at + more, i] = scores[more * size : (more + 1) * size]
            top[:, where] = jnp.maximum(top[:, where], jnp.max(scores, axis=0, keepdims=True))
        return carry

    def second_pass(at, carry, several=1):
        values = jnp.concatenate([columns(at + i, slice(HD, 2 * HD)) for i in range(several)], axis=0)
        for i in range(len(q_refs)):
            where = slice(i * lanes, (i + 1) * lanes)
            peak = jnp.maximum(top[:, where], 0.1 * LOWEST) * FACTOR
            scores = jnp.concatenate([kept[at + more, i] for more in range(several)], axis=0)
            weights = jnp.exp2(scores * FACTOR - peak)
            total[:, where] = total[:, where] + jnp.sum(weights, axis=0, keepdims=True)
            acc[:, where] = acc[:, where] + lax.dot_general(
                values, weights.astype(jnp.bfloat16), (((0,), (0,)), ((), ())), preferred_element_type=jnp.float32
            )
        return carry

    tiles = jnp.clip(lax.div(last_start - k_base + tile - 1, tile), low_tile, high_tile)
    ends = jnp.clip(lax.div(q_low + 1 - k_base, tile), tiles, high_tile)
    lax.fori_loop(low_tile, tiles, lambda at, carry: score(at, True, 1, carry), 0)
    whole_pairs = lax.div(ends - tiles, 2)
    lax.fori_loop(0, whole_pairs, lambda i, carry: score(tiles + 2 * i, False, 2, carry), 0)

    @pl.when(tiles + 2 * whole_pairs < ends)
    def _():
        score(ends - 1, False, 1, 0)

    lax.fori_loop(ends, high_tile, lambda at, carry: score(at, True, 1, carry), 0)
    pairs = lax.div(high_tile - low_tile, 2)
    lax.fori_loop(0, pairs, lambda i, carry: second_pass(low_tile + 2 * i, carry, 2), 0)

    @pl.when(low_tile + 2 * pairs < high_tile)
    def _():
        second_pass(high_tile - 1, 0)


def split_three(value):
    high = value.astype(jnp.bfloat16)
    rest = value - high.astype(jnp.float32)
    middle = rest.astype(jnp.bfloat16)
    low = (rest - middle.astype(jnp.float32)).astype(jnp.bfloat16)
    return [high, middle, low]


def pick_pages(plan_ref, mine_ref, other_ref, pages_ref):
    rows = mine_ref.shape[1]
    for i in range(pages_ref.shape[0]):
        code = plan_ref[PLAN_PAGES, i]
        own = lax.rem(code, 2) == 1
        place = lax.div(code, 2)
        chip = lax.div(place, rows)
        row = pl.multiple_of(lax.rem(place, rows), PAGE)
        for half in range(2):
            cols = slice(half * HD, (half + 1) * HD)
            pages_ref[i, half] = jnp.where(
                own, mine_ref[chip, pl.ds(row, PAGE), cols], other_ref[chip, pl.ds(row, PAGE), cols]
            )


def later_kernel(
    plan_ref, q_ref, mate_ref, mine_ref, other_ref, part_ref, pages_ref, acc, top, total, kept, picked, sem
):
    pick_pages(plan_ref, mine_ref, other_ref, picked)
    leave = pltpu.make_async_copy(picked, pages_ref, sem)
    leave.start()
    q_bases, k_base, core = bases(mine_ref.shape[1], 1)
    blocks = ((mine_ref, core), (other_ref, 1 - core))
    scan_keys(plan_ref, (2, 3), (q_ref, mate_ref), blocks, q_bases, k_base, acc, top, total, kept)
    part_ref[0:HD, :] = (acc[...] / jnp.maximum(total[...], 1e-30)).astype(jnp.bfloat16)
    stats = split_three(top[...]) + split_three(total[...])
    stats.append(jnp.zeros((STAT_ROWS - len(stats), acc.shape[1]), jnp.bfloat16))
    part_ref[HD : HD + STAT_ROWS, :] = jnp.concatenate(stats, axis=0)
    leave.wait()


def join(acc, top, total, part_ref, which, out_ref):
    rows = out_ref.shape[0]
    lanes = acc.shape[1]
    at = slice(which * lanes, (which + 1) * lanes)
    part = part_ref[0:HD, at].astype(jnp.float32)
    stats = part_ref[HD : HD + STAT_ROWS, at].astype(jnp.float32)
    part_total = stats[3:4] + stats[4:5] + stats[5:6]
    part_top = jnp.where(part_total > 0.0, stats[0:1] + stats[1:2] + stats[2:3], LOWEST)
    peak = jnp.maximum(top[...], part_top)
    own = jnp.exp2((top[...] - peak) * FACTOR)
    weight = jnp.where(part_total > 0.0, jnp.exp2((part_top - peak) * FACTOR) * part_total, 0.0)
    inverse = 1.0 / (total[...] * own + weight)
    mixed = acc[...] * (own * inverse) + part * (weight * inverse)
    for h in range(lanes // rows):
        out_ref[:, h * HD : (h + 1) * HD] = jnp.transpose(mixed[:, h * rows : (h + 1) * rows]).astype(jnp.bfloat16)


def mate_kernel(plan_ref, q_ref, mine_ref, other_ref, acc, top, total, kept):
    q_bases, k_base, core = bases(mine_ref.shape[1], 0)
    blocks = ((mine_ref, core), (other_ref, 1 - core))
    scan_keys(plan_ref, (1,), (q_ref,), blocks, q_bases[1:], k_base, acc, top, total, kept)


def mate_join_kernel(acc, top, total, part_ref, out_ref):
    join(acc, top, total, part_ref, 1, out_ref)


def own_kernel(plan_ref, q_ref, mine_ref, other_ref, part_ref, out_ref, acc, top, total, kept, turned):
    turn(q_ref, lax.rem(lax.div(lax.axis_index("kv"), 2), 2), turned)
    q_bases, k_base, core = bases(mine_ref.shape[1], 0)
    blocks = ((mine_ref, core), (other_ref, 1 - core))
    scan_keys(plan_ref, (0,), (turned,), blocks, q_bases[:1], k_base, acc, top, total, kept)
    join(acc, top, total, part_ref, 0, out_ref)


def place_kernel(own_ref, mate_ref, pages_ref, out_ref, pool_ref):
    group = lax.rem(lax.div(lax.axis_index("kv"), 2), 2)
    width = own_ref.shape[1]
    out_ref[:, pl.ds(pl.multiple_of(group * width, HD), width)] = own_ref[...]
    out_ref[:, pl.ds(pl.multiple_of((1 - group) * width, HD), width)] = mate_ref[...]
    slots = pool_ref.shape[0]
    for i in range(pages_ref.shape[0] // slots):
        pool_ref[:, :, :, i * HD : (i + 1) * HD] = pages_ref[i * slots : (i + 1) * slots]


SMEM = pl.BlockSpec(memory_space=pltpu.SMEM)
VMEM = pl.BlockSpec(memory_space=pltpu.VMEM)
ANY = pl.BlockSpec(memory_space=pl.ANY)
MIB = 1 << 20


def call(kernel, out_shape, in_specs, name, flops, scratch=(), vmem=40 * MIB, out=None):
    several = isinstance(out_shape, tuple)
    return pl.pallas_call(
        kernel,
        out_shape=out_shape,
        in_specs=in_specs,
        out_specs=out or ((VMEM,) * len(out_shape) if several else VMEM),
        scratch_shapes=scratch,
        compiler_params=pltpu.CompilerParams(vmem_limit_bytes=vmem),
        cost_estimate=pl.CostEstimate(flops=flops, bytes_accessed=3 << 20, transcendentals=0),
        name=name,
    )


def body(queries, keys, values, doc_lengths, page_table):
    rows = queries.shape[0]
    n_head = lax.axis_size("head")
    n_pb = lax.axis_size("pb")
    n_kv = lax.axis_size("kv")
    chips = n_kv // 2
    columns = queries.shape[1]
    lanes = columns // HD * rows // 2
    n_slots = rows // PAGE * 2
    shape = jax.ShapeDtypeStruct
    to_mate = [(i, i ^ 2) for i in range(n_kv)]

    local = [pltpu.VMEM(keys.shape, jnp.bfloat16)] * 2 + [pltpu.VMEM((2, rows, 2 * HD), jnp.bfloat16)]
    sent = call(
        spread_kernel, shape((chips, rows, 2 * HD), jnp.bfloat16), [ANY] * 2, "spread_keys", 1 << 10,
        local + [pltpu.SemaphoreType.DMA((2 + chips,))], 60 * MIB, ANY,
    )(keys, values)
    ring = [[2 * i + core for i in range(chips)] for core in range(2)]
    mine = lax.all_to_all(sent, "kv", 0, 0, tiled=True, axis_index_groups=ring)
    half = shape((HD, lanes), jnp.bfloat16)
    plan = shape((PLAN_PAGES + 1, rows), jnp.int32)
    turn = functools.partial(turn_kernel, n_slots=n_slots)
    keep, give, plan = call(turn, (half, half, plan), [SMEM, SMEM, VMEM], "turn_queries", 1 << 20)(
        doc_lengths, page_table, queries
    )
    mate = lax.ppermute(give, "kv", to_mate)
    later = lax.ppermute(keep, "pb", [(i + 1, i) for i in range(n_pb - 1)])
    steps = [((z + 1) * n_kv + (i ^ 2), z * n_kv + i) for z in range(n_pb - 1) for i in range(n_kv)]
    later_mate = lax.ppermute(give, ("pb", "kv"), steps)
    mine, later, later_mate = lax.optimization_barrier((mine, later, later_mate))
    other = lax.ppermute(mine, "kv", [(i, i ^ 1) for i in range(n_kv)])

    def scratch(sets):
        state = [(HD, sets * lanes), (1, sets * lanes), (1, sets * lanes)]
        kept = pltpu.VMEM((chips // SPAN, sets, 2 * rows * SPAN, lanes), jnp.float32)
        return [shape(one, jnp.float32) for one in state], [pltpu.VMEM(one, jnp.float32) for one in state], kept

    _, state, kept = scratch(2)
    part, pages = call(
        later_kernel,
        (shape((HD + STAT_ROWS, 2 * lanes), jnp.bfloat16), shape((n_slots, 2, PAGE, HD), jnp.bfloat16)),
        [VMEM] * 5, "later_rows", LONG,
        state + [kept, pltpu.VMEM((n_slots, 2, PAGE, HD), jnp.bfloat16), pltpu.SemaphoreType.DMA], out=(VMEM, ANY),
    )(plan, later, later_mate, mine, other)
    back = lax.ppermute(part, "pb", [(i, i + 1) for i in range(n_pb - 1)])
    sharing = [
        [head * n_kv + (2 * pair + chip) * 2 + core for head in range(n_head) for chip in range(2)]
        for pair in range(chips // 2)
        for core in range(2)
    ]
    arrived = lax.all_to_all(pages, ("head", "kv"), 0, 0, tiled=True, axis_index_groups=sharing)
    shapes, state, kept = scratch(1)
    out = shape((rows, columns // 2), jnp.bfloat16)
    mate_own = call(mate_kernel, tuple(shapes), [VMEM] * 4, "mate_row", LONG, [kept])(
        plan, mate, mine, other
    )
    mate_out = call(mate_join_kernel, out, [VMEM] * 4, "mate_join", 1 << 20)(*mate_own, back)
    mate_out = lax.ppermute(mate_out, "kv", to_mate)
    own_out = call(own_kernel, out, [VMEM] * 5, "own_row", 1 << 30, state + [kept, pltpu.VMEM((HD, lanes), jnp.bfloat16)])(
        plan, queries, mine, other, back
    )
    pool = shape((n_slots // (2 * n_head), 2, PAGE, 2 * n_head * HD), jnp.bfloat16)
    return call(
        place_kernel, (shape((rows, columns), jnp.bfloat16), pool), [VMEM] * 3, "place", 1 << 10
    )(own_out, mate_out, arrived)


def solution(mesh):
    in_specs = (P(("pb", "kv"), "head"), P(("pb", "kv"), "head"), P(("pb", "kv"), "head"), P(), P())
    out_specs = (P(("pb", "kv"), "head"), P(("head", "pb", "kv"), None, None, None))
    return jax.shard_map(body, mesh=mesh, in_specs=in_specs, out_specs=out_specs, check_vma=False)
```

```python
import functools
import math

import jax
import jax.numpy as jnp
from jax import lax
from jax.experimental import pallas as pl
from jax.experimental.pallas import tpu as pltpu
from jax.sharding import PartitionSpec as P

HD = 128
PAGE = 16
SPAN = 2
LOWEST = -1e30
STAT_ROWS = 16
PLAN_PAGES = 7
LONG = 10**11
FACTOR = HD**-0.5 * math.log2(math.e)


def doc_start(lengths_ref, position):
    bound = jnp.int32(0)
    start = jnp.zeros_like(position)
    for i in range(lengths_ref.shape[0]):
        bound = bound + lengths_ref[i]
        start = jnp.where(bound <= position, bound, start)
    return start


def spread_kernel(keys_ref, values_ref, out_ref, keys, values, both, sems):
    loads = [
        pltpu.make_async_copy(keys_ref, keys, sems.at[0]),
        pltpu.make_async_copy(values_ref, values, sems.at[1]),
    ]
    for copy in loads:
        copy.start()
    for copy in loads:
        copy.wait()
    copies = []
    for group in range(2):
        cols = slice(group * HD, (group + 1) * HD)
        both[group, :, 0:HD] = keys[:, cols]
        both[group, :, HD : 2 * HD] = values[:, cols]
        for chip in range(group, out_ref.shape[0], 2):
            copies.append(pltpu.make_async_copy(both.at[group], out_ref.at[chip], sems.at[2 + chip]))
            copies[-1].start()
    for copy in copies:
        copy.wait()


def bases(rows, later):
    pb, kv = lax.axis_index("pb"), lax.axis_index("kv")
    row_tokens = lax.axis_size("kv") * rows
    chip = lax.div(kv, 2)
    mate = (chip + 1 - 2 * lax.rem(chip, 2)) * 2 + lax.rem(kv, 2)
    q_row = (pb + later) * row_tokens
    return (q_row + kv * rows, q_row + mate * rows), pb * row_tokens, lax.rem(kv, 2)


def page_codes(table_ref, rows, n_slots):
    pb, kv = lax.axis_index("pb"), lax.axis_index("kv")
    n_head, n_pb, n_kv = lax.axis_size("head"), lax.axis_size("pb"), lax.axis_size("kv")
    row_pages = n_kv * rows // PAGE
    slot_rows = row_pages // n_head
    per = n_slots // (2 * n_head)
    first_chip = lax.div(kv, 4) * 2
    block_pages = rows // PAGE
    for i in range(n_slots):
        head, chip, which = i // (2 * per), i // per % 2, i % per
        slot = head * (n_pb * slot_rows) + pb * slot_rows + ((first_chip + chip) * 2 + lax.rem(kv, 2)) * per + which
        page = table_ref[slot] - pb * row_pages
        block = lax.div(page, block_pages)
        row = lax.div(block, 2) * rows + lax.rem(page, block_pages) * PAGE
        yield 2 * row + (lax.rem(block, 2) == lax.rem(kv, 2)).astype(jnp.int32)


def beside_kernel(left_ref, right_ref, out_ref):
    lanes = left_ref.shape[1]
    out_ref[:, :lanes] = left_ref[...]
    out_ref[:, lanes:] = right_ref[...]


def turn(q_ref, group, out_ref):
    rows = q_ref.shape[0]
    heads = out_ref.shape[1] // rows
    for h in range(heads):
        cols = pl.ds(pl.multiple_of((group * heads + h) * HD, HD), HD)
        out_ref[:, h * rows : (h + 1) * rows] = jnp.transpose(q_ref[:, cols])


def turn_kernel(lengths_ref, table_ref, q_ref, keep_ref, give_ref, plan_ref, *, n_slots):
    group = lax.rem(lax.div(lax.axis_index("kv"), 2), 2)
    rows = q_ref.shape[0]
    turn(q_ref, group, keep_ref)
    turn(q_ref, 1 - group, give_ref)
    lane = lax.broadcasted_iota(jnp.int32, (1, rows), 1)
    plan = [doc_start(lengths_ref, base + lane) for later in range(2) for base in bases(rows, later)[0]]
    pages = jnp.zeros((1, rows), jnp.int32)
    for i, code in enumerate(page_codes(table_ref, rows, n_slots)):
        pages = jnp.where(lane == i, code, pages)
    plan += [pages] * (plan_ref.shape[0] - len(plan))
    plan_ref[...] = jnp.concatenate(plan, axis=0)


def scan_keys(plan_ref, sets, q_ref, blocks, q_bases, k_base, acc, top, total, kept):
    rows = plan_ref.shape[1]
    lanes = q_ref.shape[1] // len(sets)
    heads = lanes // rows
    tile = 2 * rows * SPAN
    count = blocks[0][0].shape[0] // SPAN
    size = len(blocks) * rows * SPAN
    acc[...] = jnp.zeros_like(acc)
    top[...] = jnp.full_like(top, LOWEST)
    total[...] = jnp.zeros_like(total)
    q_low = functools.reduce(jnp.minimum, q_bases)
    q_high = functools.reduce(jnp.maximum, q_bases) + rows - 1
    first_start = functools.reduce(jnp.minimum, [plan_ref[i, 0] for i in sets])
    last_start = functools.reduce(jnp.maximum, [plan_ref[i, rows - 1] for i in sets])
    q_pos = [base + lax.broadcasted_iota(jnp.int32, (1, rows), 1) for base in q_bases]
    q_start = [plan_ref[i : i + 1, :] for i in sets]
    low_tile = jnp.clip(lax.div(first_start - k_base, tile), 0, count)
    high_tile = jnp.clip(lax.div(q_high - k_base, tile) + 1, 0, count)

    def columns(at, cols):
        parts = [ref[at * SPAN + chip, :, cols] for chip in range(SPAN) for ref, _ in blocks]
        return jnp.concatenate(parts, axis=0)

    def score(at, masked, several, carry):
        keys = jnp.concatenate([columns(at + i, slice(0, HD)) for i in range(several)], axis=0)
        if masked:
            row = k_base + at * tile + lax.broadcasted_iota(jnp.int32, (rows, rows), 0)
            k_pos = [row + (2 * chip + core) * rows for chip in range(SPAN) for _, core in blocks]
            k_pos = jnp.concatenate(k_pos, axis=0)
        for i in range(len(sets)):
            where = slice(i * lanes, (i + 1) * lanes)
            scores = jnp.dot(keys, q_ref[:, where], preferred_element_type=jnp.float32)
            if masked:
                seen = (k_pos <= q_pos[i]) & (k_pos >= q_start[i])
                scores = jnp.where(jnp.concatenate([seen] * heads, axis=1), scores, LOWEST)
            for more in range(several):
                kept[at + more, i] = scores[more * size : (more + 1) * size]
            top[:, where] = jnp.maximum(top[:, where], jnp.max(scores, axis=0, keepdims=True))
        return carry

    def second_pass(at, carry, several=1):
        values = jnp.concatenate([columns(at + i, slice(HD, 2 * HD)) for i in range(several)], axis=0)
        for i in range(len(sets)):
            where = slice(i * lanes, (i + 1) * lanes)
            peak = jnp.maximum(top[:, where], 0.1 * LOWEST) * FACTOR
            scores = jnp.concatenate([kept[at + more, i] for more in range(several)], axis=0)
            weights = jnp.exp2(scores * FACTOR - peak)
            total[:, where] = total[:, where] + jnp.sum(weights, axis=0, keepdims=True)
            acc[:, where] = acc[:, where] + lax.dot_general(
                values, weights.astype(jnp.bfloat16), (((0,), (0,)), ((), ())), preferred_element_type=jnp.float32
            )
        return carry

    tiles = jnp.clip(lax.div(last_start - k_base + tile - 1, tile), low_tile, high_tile)
    ends = jnp.clip(lax.div(q_low + 1 - k_base, tile), tiles, high_tile)
    lax.fori_loop(low_tile, tiles, lambda at, carry: score(at, True, 1, carry), 0)
    whole_pairs = lax.div(ends - tiles, 2)
    lax.fori_loop(0, whole_pairs, lambda i, carry: score(tiles + 2 * i, False, 2, carry), 0)

    @pl.when(tiles + 2 * whole_pairs < ends)
    def _():
        score(ends - 1, False, 1, 0)

    lax.fori_loop(ends, high_tile, lambda at, carry: score(at, True, 1, carry), 0)
    pairs = lax.div(high_tile - low_tile, 2)
    lax.fori_loop(0, pairs, lambda i, carry: second_pass(low_tile + 2 * i, carry, 2), 0)

    @pl.when(low_tile + 2 * pairs < high_tile)
    def _():
        second_pass(high_tile - 1, 0)


def split_three(value):
    high = value.astype(jnp.bfloat16)
    rest = value - high.astype(jnp.float32)
    middle = rest.astype(jnp.bfloat16)
    low = (rest - middle.astype(jnp.float32)).astype(jnp.bfloat16)
    return [high, middle, low]


def pick_pages(plan_ref, mine_ref, other_ref, pages_ref):
    rows = mine_ref.shape[1]
    for i in range(pages_ref.shape[0]):
        code = plan_ref[PLAN_PAGES, i]
        own = lax.rem(code, 2) == 1
        place = lax.div(code, 2)
        chip = lax.div(place, rows)
        row = pl.multiple_of(lax.rem(place, rows), PAGE)
        for half in range(2):
            cols = slice(half * HD, (half + 1) * HD)
            pages_ref[i, half] = jnp.where(
                own, mine_ref[chip, pl.ds(row, PAGE), cols], other_ref[chip, pl.ds(row, PAGE), cols]
            )


def later_kernel(
    plan_ref, q_ref, mine_ref, other_ref, part_ref, pages_ref, acc, top, total, kept, picked, sem
):
    pick_pages(plan_ref, mine_ref, other_ref, picked)
    leave = pltpu.make_async_copy(picked, pages_ref, sem)
    leave.start()
    q_bases, k_base, core = bases(mine_ref.shape[1], 1)
    blocks = ((mine_ref, core), (other_ref, 1 - core))
    scan_keys(plan_ref, (2, 3), q_ref, blocks, q_bases, k_base, acc, top, total, kept)
    part_ref[0:HD, :] = (acc[...] / jnp.maximum(total[...], 1e-30)).astype(jnp.bfloat16)
    stats = split_three(top[...]) + split_three(total[...])
    stats.append(jnp.zeros((STAT_ROWS - len(stats), acc.shape[1]), jnp.bfloat16))
    part_ref[HD : HD + STAT_ROWS, :] = jnp.concatenate(stats, axis=0)
    leave.wait()


def join(acc, top, total, part_ref, which, out_ref):
    rows = out_ref.shape[0]
    lanes = acc.shape[1]
    at = slice(which * lanes, (which + 1) * lanes)
    part = part_ref[0:HD, at].astype(jnp.float32)
    stats = part_ref[HD : HD + STAT_ROWS, at].astype(jnp.float32)
    part_total = stats[3:4] + stats[4:5] + stats[5:6]
    part_top = jnp.where(part_total > 0.0, stats[0:1] + stats[1:2] + stats[2:3], LOWEST)
    peak = jnp.maximum(top[...], part_top)
    own = jnp.exp2((top[...] - peak) * FACTOR)
    weight = jnp.where(part_total > 0.0, jnp.exp2((part_top - peak) * FACTOR) * part_total, 0.0)
    inverse = 1.0 / (total[...] * own + weight)
    mixed = acc[...] * (own * inverse) + part * (weight * inverse)
    for h in range(lanes // rows):
        out_ref[:, h * HD : (h + 1) * HD] = jnp.transpose(mixed[:, h * rows : (h + 1) * rows]).astype(jnp.bfloat16)


def mate_kernel(plan_ref, q_ref, mine_ref, other_ref, acc, top, total, kept):
    q_bases, k_base, core = bases(mine_ref.shape[1], 0)
    blocks = ((mine_ref, core), (other_ref, 1 - core))
    scan_keys(plan_ref, (1,), q_ref, blocks, q_bases[1:], k_base, acc, top, total, kept)


def mate_join_kernel(acc, top, total, part_ref, out_ref):
    join(acc, top, total, part_ref, 1, out_ref)


def own_kernel(plan_ref, q_ref, mine_ref, other_ref, part_ref, out_ref, acc, top, total, kept, turned):
    turn(q_ref, lax.rem(lax.div(lax.axis_index("kv"), 2), 2), turned)
    q_bases, k_base, core = bases(mine_ref.shape[1], 0)
    blocks = ((mine_ref, core), (other_ref, 1 - core))
    scan_keys(plan_ref, (0,), turned, blocks, q_bases[:1], k_base, acc, top, total, kept)
    join(acc, top, total, part_ref, 0, out_ref)


def place_kernel(own_ref, mate_ref, pages_ref, out_ref, pool_ref):
    group = lax.rem(lax.div(lax.axis_index("kv"), 2), 2)
    width = own_ref.shape[1]
    out_ref[:, pl.ds(pl.multiple_of(group * width, HD), width)] = own_ref[...]
    out_ref[:, pl.ds(pl.multiple_of((1 - group) * width, HD), width)] = mate_ref[...]
    slots = pool_ref.shape[0]
    for i in range(pages_ref.shape[0] // slots):
        pool_ref[:, :, :, i * HD : (i + 1) * HD] = pages_ref[i * slots : (i + 1) * slots]


SMEM = pl.BlockSpec(memory_space=pltpu.SMEM)
VMEM = pl.BlockSpec(memory_space=pltpu.VMEM)
ANY = pl.BlockSpec(memory_space=pl.ANY)
MIB = 1 << 20


def call(kernel, out_shape, in_specs, name, flops, scratch=(), vmem=40 * MIB, out=None):
    several = isinstance(out_shape, tuple)
    return pl.pallas_call(
        kernel,
        out_shape=out_shape,
        in_specs=in_specs,
        out_specs=out or ((VMEM,) * len(out_shape) if several else VMEM),
        scratch_shapes=scratch,
        compiler_params=pltpu.CompilerParams(vmem_limit_bytes=vmem),
        cost_estimate=pl.CostEstimate(flops=flops, bytes_accessed=3 << 20, transcendentals=0),
        name=name,
    )


def body(queries, keys, values, doc_lengths, page_table):
    rows = queries.shape[0]
    n_head = lax.axis_size("head")
    n_pb = lax.axis_size("pb")
    n_kv = lax.axis_size("kv")
    chips = n_kv // 2
    columns = queries.shape[1]
    lanes = columns // HD * rows // 2
    n_slots = rows // PAGE * 2
    shape = jax.ShapeDtypeStruct
    to_mate = [(i, i ^ 2) for i in range(n_kv)]

    local = [pltpu.VMEM(keys.shape, jnp.bfloat16)] * 2 + [pltpu.VMEM((2, rows, 2 * HD), jnp.bfloat16)]
    sent = call(
        spread_kernel, shape((chips, rows, 2 * HD), jnp.bfloat16), [ANY] * 2, "spread_keys", 1 << 10,
        local + [pltpu.SemaphoreType.DMA((2 + chips,))], 60 * MIB, ANY,
    )(keys, values)
    ring = [[2 * i + core for i in range(chips)] for core in range(2)]
    mine = lax.all_to_all(sent, "kv", 0, 0, tiled=True, axis_index_groups=ring)
    half = shape((HD, lanes), jnp.bfloat16)
    plan = shape((PLAN_PAGES + 1, rows), jnp.int32)
    turn = functools.partial(turn_kernel, n_slots=n_slots)
    keep, give, plan = call(turn, (half, half, plan), [SMEM, SMEM, VMEM], "turn_queries", 1 << 20)(
        doc_lengths, page_table, queries
    )
    mate = lax.ppermute(give, "kv", to_mate)
    later = lax.ppermute(keep, "pb", [(i + 1, i) for i in range(n_pb - 1)])
    steps = [((z + 1) * n_kv + (i ^ 2), z * n_kv + i) for z in range(n_pb - 1) for i in range(n_kv)]
    later_mate = lax.ppermute(give, ("pb", "kv"), steps)
    mine, later = lax.optimization_barrier((mine, later))
    later = call(beside_kernel, shape((HD, 2 * lanes), jnp.bfloat16), [VMEM] * 2, "beside", LONG)(later, later_mate)
    other = lax.ppermute(mine, "kv", [(i, i ^ 1) for i in range(n_kv)])

    def scratch(sets):
        state = [(HD, sets * lanes), (1, sets * lanes), (1, sets * lanes)]
        kept = pltpu.VMEM((chips // SPAN, sets, 2 * rows * SPAN, lanes), jnp.float32)
        return [shape(one, jnp.float32) for one in state], [pltpu.VMEM(one, jnp.float32) for one in state], kept

    _, state, kept = scratch(2)
    part, pages = call(
        later_kernel,
        (shape((HD + STAT_ROWS, 2 * lanes), jnp.bfloat16), shape((n_slots, 2, PAGE, HD), jnp.bfloat16)),
        [VMEM] * 4, "later_rows", LONG,
        state + [kept, pltpu.VMEM((n_slots, 2, PAGE, HD), jnp.bfloat16), pltpu.SemaphoreType.DMA], out=(VMEM, ANY),
    )(plan, later, mine, other)
    back = lax.ppermute(part, "pb", [(i, i + 1) for i in range(n_pb - 1)])
    sharing = [
        [head * n_kv + (2 * pair + chip) * 2 + core for head in range(n_head) for chip in range(2)]
        for pair in range(chips // 2)
        for core in range(2)
    ]
    arrived = lax.all_to_all(pages, ("head", "kv"), 0, 0, tiled=True, axis_index_groups=sharing)
    shapes, state, kept = scratch(1)
    out = shape((rows, columns // 2), jnp.bfloat16)
    mate_own = call(mate_kernel, tuple(shapes), [VMEM] * 4, "mate_row", LONG, [kept])(
        plan, mate, mine, other
    )
    mate_out = call(mate_join_kernel, out, [VMEM] * 4, "mate_join", 1 << 20)(*mate_own, back)
    mate_out = lax.ppermute(mate_out, "kv", to_mate)
    own_out = call(own_kernel, out, [VMEM] * 5, "own_row", 1 << 30, state + [kept, pltpu.VMEM((HD, lanes), jnp.bfloat16)])(
        plan, queries, mine, other, back
    )
    pool = shape((n_slots // (2 * n_head), 2, PAGE, 2 * n_head * HD), jnp.bfloat16)
    return call(
        place_kernel, (shape((rows, columns), jnp.bfloat16), pool), [VMEM] * 3, "place", 1 << 10
    )(own_out, mate_out, arrived)


def solution(mesh):
    in_specs = (P(("pb", "kv"), "head"), P(("pb", "kv"), "head"), P(("pb", "kv"), "head"), P(), P())
    out_specs = (P(("pb", "kv"), "head"), P(("head", "pb", "kv"), None, None, None))
    return jax.shard_map(body, mesh=mesh, in_specs=in_specs, out_specs=out_specs, check_vma=False)
```

```python
import functools
import math

import jax
import jax.numpy as jnp
from jax import lax
from jax.experimental import pallas as pl
from jax.experimental.pallas import tpu as pltpu
from jax.sharding import PartitionSpec as P

HD = 128
PAGE = 16
SPAN = 2
LOWEST = -1e30
STAT_ROWS = 16
PLAN_PAGES = 7
LONG = 10**11
FACTOR = HD**-0.5 * math.log2(math.e)


def doc_start(lengths_ref, position):
    bound = jnp.int32(0)
    start = jnp.zeros_like(position)
    for i in range(lengths_ref.shape[0]):
        bound = bound + lengths_ref[i]
        start = jnp.where(bound <= position, bound, start)
    return start


def spread_kernel(keys_ref, values_ref, out_ref, keys, values, both, sems):
    loads = [
        pltpu.make_async_copy(keys_ref, keys, sems.at[0]),
        pltpu.make_async_copy(values_ref, values, sems.at[1]),
    ]
    for copy in loads:
        copy.start()
    for copy in loads:
        copy.wait()
    copies = []
    for group in range(2):
        cols = slice(group * HD, (group + 1) * HD)
        both[group, :, 0:HD] = keys[:, cols]
        both[group, :, HD : 2 * HD] = values[:, cols]
        for chip in range(group, out_ref.shape[0], 2):
            copies.append(pltpu.make_async_copy(both.at[group], out_ref.at[chip], sems.at[2 + chip]))
            copies[-1].start()
    for copy in copies:
        copy.wait()


def bases(rows, later):
    pb, kv = lax.axis_index("pb"), lax.axis_index("kv")
    row_tokens = lax.axis_size("kv") * rows
    chip = lax.div(kv, 2)
    mate = (chip + 1 - 2 * lax.rem(chip, 2)) * 2 + lax.rem(kv, 2)
    q_row = (pb + later) * row_tokens
    return (q_row + kv * rows, q_row + mate * rows), pb * row_tokens, lax.rem(kv, 2)


def page_codes(table_ref, rows, n_slots):
    pb, kv = lax.axis_index("pb"), lax.axis_index("kv")
    n_head, n_pb, n_kv = lax.axis_size("head"), lax.axis_size("pb"), lax.axis_size("kv")
    row_pages = n_kv * rows // PAGE
    slot_rows = row_pages // n_head
    per = n_slots // (2 * n_head)
    first_chip = lax.div(kv, 4) * 2
    block_pages = rows // PAGE
    for i in range(n_slots):
        head, chip, which = i // (2 * per), i // per % 2, i % per
        slot = head * (n_pb * slot_rows) + pb * slot_rows + ((first_chip + chip) * 2 + lax.rem(kv, 2)) * per + which
        page = table_ref[slot] - pb * row_pages
        block = lax.div(page, block_pages)
        row = lax.div(block, 2) * rows + lax.rem(page, block_pages) * PAGE
        yield 2 * row + (lax.rem(block, 2) == lax.rem(kv, 2)).astype(jnp.int32)


def beside_kernel(left_ref, right_ref, out_ref):
    lanes = left_ref.shape[1]
    out_ref[:, :lanes] = left_ref[...]
    out_ref[:, lanes:] = right_ref[...]


def turn(q_ref, group, out_ref):
    rows = q_ref.shape[0]
    heads = out_ref.shape[1] // rows
    for h in range(heads):
        cols = pl.ds(pl.multiple_of((group * heads + h) * HD, HD), HD)
        out_ref[:, h * rows : (h + 1) * rows] = jnp.transpose(q_ref[:, cols])


def turn_kernel(lengths_ref, table_ref, q_ref, keep_ref, give_ref, plan_ref, *, n_slots):
    group = lax.rem(lax.div(lax.axis_index("kv"), 2), 2)
    rows = q_ref.shape[0]
    turn(q_ref, group, keep_ref)
    turn(q_ref, 1 - group, give_ref)
    lane = lax.broadcasted_iota(jnp.int32, (1, rows), 1)
    plan = [doc_start(lengths_ref, base + lane) for later in range(2) for base in bases(rows, later)[0]]
    pages = jnp.zeros((1, rows), jnp.int32)
    for i, code in enumerate(page_codes(table_ref, rows, n_slots)):
        pages = jnp.where(lane == i, code, pages)
    plan += [pages] * (plan_ref.shape[0] - len(plan))
    plan_ref[...] = jnp.concatenate(plan, axis=0)


def scan_keys(plan_ref, sets, q_ref, blocks, q_bases, k_base, acc, top, total, kept):
    rows = plan_ref.shape[1]
    lanes = q_ref.shape[1] // len(sets)
    heads = lanes // rows
    tile = 2 * rows * SPAN
    count = blocks[0][0].shape[0] // SPAN
    size = len(blocks) * rows * SPAN
    acc[...] = jnp.zeros_like(acc)
    top[...] = jnp.full_like(top, LOWEST)
    total[...] = jnp.zeros_like(total)
    q_low = functools.reduce(jnp.minimum, q_bases)
    q_high = functools.reduce(jnp.maximum, q_bases) + rows - 1
    first_start = functools.reduce(jnp.minimum, [plan_ref[i, 0] for i in sets])
    last_start = functools.reduce(jnp.maximum, [plan_ref[i, rows - 1] for i in sets])
    q_pos = [base + lax.broadcasted_iota(jnp.int32, (1, rows), 1) for base in q_bases]
    q_start = [plan_ref[i : i + 1, :] for i in sets]
    low_tile = jnp.clip(lax.div(first_start - k_base, tile), 0, count)
    high_tile = jnp.clip(lax.div(q_high - k_base, tile) + 1, 0, count)

    def columns(at, cols):
        parts = [ref[at * SPAN + chip, :, cols] for chip in range(SPAN) for ref, _ in blocks]
        return jnp.concatenate(parts, axis=0)

    def score(at, masked, several, carry):
        keys = jnp.concatenate([columns(at + i, slice(0, HD)) for i in range(several)], axis=0)
        if masked:
            row = k_base + at * tile + lax.broadcasted_iota(jnp.int32, (rows, rows), 0)
            k_pos = [row + (2 * chip + core) * rows for chip in range(SPAN) for _, core in blocks]
            k_pos = jnp.concatenate(k_pos, axis=0)
        for i in range(len(sets)):
            where = slice(i * lanes, (i + 1) * lanes)
            scores = jnp.dot(keys, q_ref[:, where], preferred_element_type=jnp.float32)
            if masked:
                seen = (k_pos <= q_pos[i]) & (k_pos >= q_start[i])
                scores = jnp.where(jnp.concatenate([seen] * heads, axis=1), scores, LOWEST)
            for more in range(several):
                kept[at + more, i] = scores[more * size : (more + 1) * size]
            top[:, where] = jnp.maximum(top[:, where], jnp.max(scores, axis=0, keepdims=True))
        return carry

    def second_pass(at, carry, several=1):
        values = jnp.concatenate([columns(at + i, slice(HD, 2 * HD)) for i in range(several)], axis=0)
        for i in range(len(sets)):
            where = slice(i * lanes, (i + 1) * lanes)
            peak = jnp.maximum(top[:, where], 0.1 * LOWEST) * FACTOR
            scores = jnp.concatenate([kept[at + more, i] for more in range(several)], axis=0)
            weights = jnp.exp2(scores * FACTOR - peak)
            total[:, where] = total[:, where] + jnp.sum(weights, axis=0, keepdims=True)
            acc[:, where] = acc[:, where] + lax.dot_general(
                values, weights.astype(jnp.bfloat16), (((0,), (0,)), ((), ())), preferred_element_type=jnp.float32
            )
        return carry

    tiles = jnp.clip(lax.div(last_start - k_base + tile - 1, tile), low_tile, high_tile)
    ends = jnp.clip(lax.div(q_low + 1 - k_base, tile), tiles, high_tile)
    lax.fori_loop(low_tile, tiles, lambda at, carry: score(at, True, 1, carry), 0)
    whole_pairs = lax.div(ends - tiles, 2)
    lax.fori_loop(0, whole_pairs, lambda i, carry: score(tiles + 2 * i, False, 2, carry), 0)

    @pl.when(tiles + 2 * whole_pairs < ends)
    def _():
        score(ends - 1, False, 1, 0)

    lax.fori_loop(ends, high_tile, lambda at, carry: score(at, True, 1, carry), 0)
    pairs = lax.div(high_tile - low_tile, 2)
    lax.fori_loop(0, pairs, lambda i, carry: second_pass(low_tile + 2 * i, carry, 2), 0)

    @pl.when(low_tile + 2 * pairs < high_tile)
    def _():
        second_pass(high_tile - 1, 0)


def split_three(value):
    high = value.astype(jnp.bfloat16)
    rest = value - high.astype(jnp.float32)
    middle = rest.astype(jnp.bfloat16)
    low = (rest - middle.astype(jnp.float32)).astype(jnp.bfloat16)
    return [high, middle, low]


def pick_pages(plan_ref, mine_ref, other_ref, pages_ref):
    rows = mine_ref.shape[1]
    for i in range(pages_ref.shape[0]):
        code = plan_ref[PLAN_PAGES, i]
        own = lax.rem(code, 2) == 1
        place = lax.div(code, 2)
        chip = lax.div(place, rows)
        row = pl.multiple_of(lax.rem(place, rows), PAGE)
        for half in range(2):
            cols = slice(half * HD, (half + 1) * HD)
            pages_ref[i, half] = jnp.where(
                own, mine_ref[chip, pl.ds(row, PAGE), cols], other_ref[chip, pl.ds(row, PAGE), cols]
            )


def later_kernel(
    plan_ref, q_ref, mine_ref, other_ref, part_ref, pages_ref, acc, top, total, kept, picked, sem
):
    pick_pages(plan_ref, mine_ref, other_ref, picked)
    leave = pltpu.make_async_copy(picked, pages_ref, sem)
    leave.start()
    q_bases, k_base, core = bases(mine_ref.shape[1], 1)
    blocks = ((mine_ref, core), (other_ref, 1 - core))
    scan_keys(plan_ref, (2, 3), q_ref, blocks, q_bases, k_base, acc, top, total, kept)
    part_ref[0:HD, :] = (acc[...] / jnp.maximum(total[...], 1e-30)).astype(jnp.bfloat16)
    stats = split_three(top[...]) + split_three(total[...])
    stats.append(jnp.zeros((STAT_ROWS - len(stats), acc.shape[1]), jnp.bfloat16))
    part_ref[HD : HD + STAT_ROWS, :] = jnp.concatenate(stats, axis=0)
    leave.wait()


def join(acc, top, total, part_ref, which, out_ref):
    rows = out_ref.shape[0]
    lanes = acc.shape[1]
    at = slice(which * lanes, (which + 1) * lanes)
    part = part_ref[0:HD, at].astype(jnp.float32)
    stats = part_ref[HD : HD + STAT_ROWS, at].astype(jnp.float32)
    part_total = stats[3:4] + stats[4:5] + stats[5:6]
    part_top = jnp.where(part_total > 0.0, stats[0:1] + stats[1:2] + stats[2:3], LOWEST)
    peak = jnp.maximum(top[...], part_top)
    own = jnp.exp2((top[...] - peak) * FACTOR)
    weight = jnp.where(part_total > 0.0, jnp.exp2((part_top - peak) * FACTOR) * part_total, 0.0)
    inverse = 1.0 / (total[...] * own + weight)
    mixed = acc[...] * (own * inverse) + part * (weight * inverse)
    for h in range(lanes // rows):
        out_ref[:, h * HD : (h + 1) * HD] = jnp.transpose(mixed[:, h * rows : (h + 1) * rows]).astype(jnp.bfloat16)


def mate_kernel(plan_ref, q_ref, mine_ref, other_ref, acc, top, total, kept):
    q_bases, k_base, core = bases(mine_ref.shape[1], 0)
    blocks = ((mine_ref, core), (other_ref, 1 - core))
    scan_keys(plan_ref, (1,), q_ref, blocks, q_bases[1:], k_base, acc, top, total, kept)


def mate_join_kernel(acc, top, total, part_ref, out_ref):
    join(acc, top, total, part_ref, 1, out_ref)


def own_kernel(plan_ref, q_ref, mine_ref, other_ref, part_ref, out_ref, acc, top, total, kept, turned):
    turn(q_ref, lax.rem(lax.div(lax.axis_index("kv"), 2), 2), turned)
    q_bases, k_base, core = bases(mine_ref.shape[1], 0)
    blocks = ((mine_ref, core), (other_ref, 1 - core))
    scan_keys(plan_ref, (0,), turned, blocks, q_bases[:1], k_base, acc, top, total, kept)
    join(acc, top, total, part_ref, 0, out_ref)


def place_kernel(own_ref, mate_ref, pages_ref, out_ref, pool_ref):
    group = lax.rem(lax.div(lax.axis_index("kv"), 2), 2)
    width = own_ref.shape[1]
    out_ref[:, pl.ds(pl.multiple_of(group * width, HD), width)] = own_ref[...]
    out_ref[:, pl.ds(pl.multiple_of((1 - group) * width, HD), width)] = mate_ref[...]
    slots = pool_ref.shape[0]
    for i in range(pages_ref.shape[0] // slots):
        pool_ref[:, :, :, i * HD : (i + 1) * HD] = pages_ref[i * slots : (i + 1) * slots]


SMEM = pl.BlockSpec(memory_space=pltpu.SMEM)
VMEM = pl.BlockSpec(memory_space=pltpu.VMEM)
ANY = pl.BlockSpec(memory_space=pl.ANY)
MIB = 1 << 20


def call(kernel, out_shape, in_specs, name, flops, scratch=(), vmem=40 * MIB, out=None):
    several = isinstance(out_shape, tuple)
    return pl.pallas_call(
        kernel,
        out_shape=out_shape,
        in_specs=in_specs,
        out_specs=out or ((VMEM,) * len(out_shape) if several else VMEM),
        scratch_shapes=scratch,
        compiler_params=pltpu.CompilerParams(vmem_limit_bytes=vmem),
        cost_estimate=pl.CostEstimate(flops=flops, bytes_accessed=3 << 20, transcendentals=0),
        name=name,
    )


def body(queries, keys, values, doc_lengths, page_table):
    rows = queries.shape[0]
    n_head = lax.axis_size("head")
    n_pb = lax.axis_size("pb")
    n_kv = lax.axis_size("kv")
    chips = n_kv // 2
    columns = queries.shape[1]
    lanes = columns // HD * rows // 2
    n_slots = rows // PAGE * 2
    shape = jax.ShapeDtypeStruct
    to_mate = [(i, i ^ 2) for i in range(n_kv)]

    local = [pltpu.VMEM(keys.shape, jnp.bfloat16)] * 2 + [pltpu.VMEM((2, rows, 2 * HD), jnp.bfloat16)]
    sent = call(
        spread_kernel, shape((chips, rows, 2 * HD), jnp.bfloat16), [ANY] * 2, "spread_keys", 1 << 10,
        local + [pltpu.SemaphoreType.DMA((2 + chips,))], 60 * MIB, ANY,
    )(keys, values)
    ring = [[2 * i + core for i in range(chips)] for core in range(2)]
    mine = lax.all_to_all(sent, "kv", 0, 0, tiled=True, axis_index_groups=ring)
    half = shape((HD, lanes), jnp.bfloat16)
    plan = shape((PLAN_PAGES + 1, rows), jnp.int32)
    turn = functools.partial(turn_kernel, n_slots=n_slots)
    keep, give, plan = call(turn, (half, half, plan), [SMEM, SMEM, VMEM], "turn_queries", 1 << 20)(
        doc_lengths, page_table, queries
    )
    mate = lax.ppermute(give, "kv", to_mate)
    later = lax.ppermute(keep, "pb", [(i + 1, i) for i in range(n_pb - 1)])
    steps = [((z + 1) * n_kv + (i ^ 2), z * n_kv + i) for z in range(n_pb - 1) for i in range(n_kv)]
    later_mate = lax.ppermute(give, ("pb", "kv"), steps)
    later = call(beside_kernel, shape((HD, 2 * lanes), jnp.bfloat16), [VMEM] * 2, "beside", LONG)(later, later_mate)
    other = lax.ppermute(mine, "kv", [(i, i ^ 1) for i in range(n_kv)])

    def scratch(sets):
        state = [(HD, sets * lanes), (1, sets * lanes), (1, sets * lanes)]
        kept = pltpu.VMEM((chips // SPAN, sets, 2 * rows * SPAN, lanes), jnp.float32)
        return [shape(one, jnp.float32) for one in state], [pltpu.VMEM(one, jnp.float32) for one in state], kept

    _, state, kept = scratch(2)
    part, pages = call(
        later_kernel,
        (shape((HD + STAT_ROWS, 2 * lanes), jnp.bfloat16), shape((n_slots, 2, PAGE, HD), jnp.bfloat16)),
        [VMEM] * 4, "later_rows", LONG,
        state + [kept, pltpu.VMEM((n_slots, 2, PAGE, HD), jnp.bfloat16), pltpu.SemaphoreType.DMA], out=(VMEM, ANY),
    )(plan, later, mine, other)
    back = lax.ppermute(part, "pb", [(i, i + 1) for i in range(n_pb - 1)])
    sharing = [
        [head * n_kv + (2 * pair + chip) * 2 + core for head in range(n_head) for chip in range(2)]
        for pair in range(chips // 2)
        for core in range(2)
    ]
    arrived = lax.all_to_all(pages, ("head", "kv"), 0, 0, tiled=True, axis_index_groups=sharing)
    shapes, state, kept = scratch(1)
    out = shape((rows, columns // 2), jnp.bfloat16)
    mate_own = call(mate_kernel, tuple(shapes), [VMEM] * 4, "mate_row", LONG, [kept])(
        plan, mate, mine, other
    )
    mate_out = call(mate_join_kernel, out, [VMEM] * 4, "mate_join", 1 << 20)(*mate_own, back)
    mate_out = lax.ppermute(mate_out, "kv", to_mate)
    own_out = call(own_kernel, out, [VMEM] * 5, "own_row", 1 << 30, state + [kept, pltpu.VMEM((HD, lanes), jnp.bfloat16)])(
        plan, queries, mine, other, back
    )
    pool = shape((n_slots // (2 * n_head), 2, PAGE, 2 * n_head * HD), jnp.bfloat16)
    return call(
        place_kernel, (shape((rows, columns), jnp.bfloat16), pool), [VMEM] * 3, "place", 1 << 10
    )(own_out, mate_out, arrived)


def solution(mesh):
    in_specs = (P(("pb", "kv"), "head"), P(("pb", "kv"), "head"), P(("pb", "kv"), "head"), P(), P())
    out_specs = (P(("pb", "kv"), "head"), P(("head", "pb", "kv"), None, None, None))
    return jax.shard_map(body, mesh=mesh, in_specs=in_specs, out_specs=out_specs, check_vma=False)
```
